512 devices in a mesh: section: 16 (over x, z_hi), dp: 32 (over z_lo, y, core).
Axes of the slice: x: 4, y: 4, z: 16 (z_hi: 4, z_lo: 4; z = z_hi * 4 + z_lo), core: 2. Of those that a mesh axis runs over, the one named last changes fastest.
Arguments:
- hidden: bfloat16 [16, 64, 4096], P('section', 'dp'), may hold values from -16 to 16
- norm_gain: float32 [4096], replicated, may hold values from 0.5 to 2
- exit_head: bfloat16 [16384, 4096], P('dp', 'section'), may hold values from -4 to 4
- targets: int32 [64], replicated, may hold values from 0 to 16383
- loss_numerators: int32 [16], replicated, may hold values from 1 to 64
- top_grad: bfloat16 [64, 4096], P('dp'), may hold values from -8 to 8
Outputs:
- grad_head: bfloat16 [16384, 4096], P('dp', 'section')
- grad_hidden: bfloat16 [16, 64, 4096], P('section', 'dp')
The draws below stay inside these ranges and needn't reach their ends.
All inputs are finite; a program needn't handle non-finite values.
Results may differ from the reference program's by a relative error of at most 0.0062.
Values may be sent and summed in bfloat16 or wider, within the bound.
A program may use at most 64 MiB of HBM per device.

```python
import math
import jax
import jax.numpy as jnp
import numpy as np
from jax import lax

D = 4096
VOCAB = 16384
ROWS = 64
EXIT_DENOM = 16
SECTIONS = 16


def shared_head(key):
    base = jax.random.normal(key, (VOCAB, D), jnp.float32)
    base = jnp.clip(base, -4.0, 4.0) * (4.0 / math.sqrt(D))
    signs = jax.random.randint(jax.random.fold_in(key, 11), (16, D), 0, 2).astype(jnp.float32) * 2.0 - 1.0
    planted = signs * (240.0 / D)
    return jnp.concatenate([planted, base[16:]], axis=0)


def draw_exit_head(key, part):
    base = shared_head(key)
    return base.astype(jnp.bfloat16)


def draw_hidden(key, part):
    head_rows = shared_head(key)[:16] * (D / 240.0)
    key = jax.random.fold_in(key, 5)
    key_noise, key_rows, key_cols = jax.random.split(key, 3)
    noise = jnp.clip(jax.random.normal(key_noise, (SECTIONS, ROWS, D), jnp.float32), -4.0, 4.0)
    row_scale = jnp.exp(jax.random.uniform(key_rows, (SECTIONS, ROWS, 1), jnp.float32, math.log(0.25), 0.0))
    col_scale = jnp.exp(jax.random.uniform(key_cols, (1, 1, D), jnp.float32, 0.0, math.log(4.0)))
    field = noise * col_scale * row_scale
    section_ids = jnp.arange(SECTIONS, dtype=jnp.int32)[:, None]
    row_ids = jnp.arange(4, dtype=jnp.int32)[None, :]
    picks = 2 * ((section_ids + row_ids) % 8)
    blend = jnp.array([1.0, 0.9, 0.75, 0.6], jnp.float32)[None, :, None]
    aligned = head_rows[picks] * blend + field[:, :4, :] * (1.0 - blend)
    field = jnp.concatenate([aligned, field[:, 4:, :]], axis=1)
    return field.astype(jnp.bfloat16)


def set_ends(values, key, low, high):
    place = [jax.random.randint(jax.random.fold_in(key, axis), (), 0, length) for axis, length in enumerate(values.shape)]
    main_axis = values.shape.index(max(values.shape))
    neighbour = place[:main_axis] + [(place[main_axis] + 1) % values.shape[main_axis]] + place[main_axis + 1:]
    return values.at[tuple(place)].set(low).at[tuple(neighbour)].set(high)


def block_levels(own_key, extent, pieces, low, high):
    gain, own = 1.0, jax.random.fold_in(own_key, 6)
    for position, blocks in pieces:
        heights = jnp.exp(jax.random.uniform(jax.random.fold_in(own, position), (blocks,), jnp.float32, low / len(pieces), high / len(pieces)))
        gain = gain * jnp.repeat(heights, extent[position] // blocks).reshape([-1 if axis == position else 1 for axis in range(len(extent))])
    return gain


def rank_bounds(number_of, lean):
    portions = [(1 << 20) // math.isqrt(grade ** lean) + 1 for grade in range(1, number_of + 1)]
    scale = 1 + sum(portions) // (1 << 30)
    return np.cumsum(np.array([max(1, weight // scale) for weight in portions]))


def skewed_ids(stream_key, extent, count, lean):
    grid = rank_bounds(count, lean)
    pick = jax.random.randint(jax.random.fold_in(stream_key, 1), extent, 0, int(grid[count - 1]))
    grade = jnp.searchsorted(jnp.asarray(grid, jnp.int32), pick, side="right")
    return jax.random.permutation(jax.random.fold_in(stream_key, 2), count)[grade].astype(jnp.int32)


def gaussian(key, extent, scale, most, cuts=(), kind=jnp.bfloat16):
    level = block_levels(key, extent, cuts, -0.22, 0.18) if cuts else 1.0
    values = jax.random.normal(key, extent, jnp.float32) * scale * level
    return jnp.minimum(jnp.maximum(values, -most), most).astype(kind)


def setup_inputs(seed: int = 0) -> dict:
    splits = jax.random.split(jax.random.key(seed), 7)
    hidden = draw_hidden(jax.random.fold_in(splits[6], 71), 0)
    norm_gain = jnp.clip(jnp.exp(jax.random.uniform(splits[1], (D,), jnp.float32, math.log(0.5), math.log(2.0))), 0.5, 2.0)
    exit_head = draw_exit_head(jax.random.fold_in(splits[6], 71), 0)
    targets = set_ends(skewed_ids(splits[3], (ROWS,), VOCAB, 1), jax.random.fold_in(splits[3], 3), 0, VOCAB - 1).astype(jnp.int32)
    loss_numerators = set_ends(jax.random.randint(splits[4], (SECTIONS,), 1, 65), jax.random.fold_in(splits[4], 1), 1, 64).astype(jnp.int32)
    top_grad = gaussian(splits[5], (ROWS, D), 2.0, 8.0, ((0, 32),))
    return {"hidden": hidden, "norm_gain": norm_gain, "exit_head": exit_head, "targets": targets, "loss_numerators": loss_numerators, "top_grad": top_grad}


EPSILON = 1e-05

def reference(hidden, norm_gain, exit_head, targets, loss_numerators, top_grad):
    hidden_f = hidden.astype(jnp.float32)
    inverse = lax.rsqrt(lax.optimization_barrier(jnp.mean(hidden_f * hidden_f, axis=-1)) + EPSILON)
    normed = (hidden_f * inverse[..., None] * norm_gain).astype(jnp.bfloat16)
    feat_part = D // SECTIONS
    head_blocks = exit_head.reshape(VOCAB, SECTIONS, feat_part).transpose(1, 0, 2)
    vocab_ids = jnp.arange(VOCAB, dtype=jnp.int32)
    onehot = (targets[:, None] == vocab_ids[None, :]).astype(jnp.float32)
    weights = loss_numerators.astype(jnp.float32) / EXIT_DENOM

    def one_section(grad_sum, inputs):
        normed_rows, weight = inputs
        row_blocks = normed_rows.reshape(ROWS, SECTIONS, feat_part).transpose(1, 0, 2)

        def add_block(logits, pair):
            rows_part, head_part = pair
            partial_logits = lax.dot_general(rows_part, head_part, (((1,), (1,)), ((), ())), preferred_element_type=jnp.float32)
            return (logits + partial_logits, None)
        logits, unused = lax.scan(add_block, jnp.zeros((ROWS, VOCAB), jnp.float32), (row_blocks, head_blocks))
        peak_val = lax.optimization_barrier(jnp.max(logits, axis=-1))
        expo = jnp.exp(logits - peak_val[:, None])
        total_exp = lax.optimization_barrier(jnp.sum(expo, axis=-1))
        dlogits = (weight * (expo / total_exp[:, None] - onehot)).astype(jnp.bfloat16)
        head_grad = lax.dot_general(dlogits, normed_rows, (((0,), (0,)), ((), ())), preferred_element_type=jnp.float32)
        feat_grads = jnp.dot(dlogits, exit_head, preferred_element_type=jnp.float32)
        return (grad_sum + head_grad, feat_grads)
    grad_sum, feat_grads = lax.scan(one_section, jnp.zeros((VOCAB, D), jnp.float32), (normed, weights))
    row_dots = lax.optimization_barrier(jnp.mean(feat_grads * norm_gain * hidden_f, axis=-1))
    exit_grads = inverse[..., None] * (norm_gain * feat_grads - hidden_f * (inverse * inverse * row_dots)[..., None])
    later_sum = jnp.flip(jnp.cumsum(jnp.flip(exit_grads, 0), axis=0), 0)
    grad_hidden = (later_sum + top_grad.astype(jnp.float32)[None]).astype(jnp.bfloat16)
    return (grad_sum.astype(jnp.bfloat16), grad_hidden)
```

```python
import functools

import jax
import jax.numpy as jnp
from jax import lax
from jax.experimental import pallas as pl
from jax.experimental.pallas import tpu as pltpu
from jax.sharding import PartitionSpec as P

MESH = pl.DeviceIdType.MESH
EXIT_DENOM = 16
EPSILON = 1e-05
F32 = jnp.float32
BF16 = jnp.bfloat16
D = 4096
HALF = D // 2
COPIES = 128


def dot(a, b, contract):
    return lax.dot_general(a, b, (contract, ((), ())), preferred_element_type=F32)


def kernel(
    hidden_ref, gain_ref, head_ref, targets_ref, nums_ref, top_ref,
    ghead_ref, ghid_ref,
    hid, hid8, inv8, n8, norm, heads, logits, stats, dlog_t, dlog_2, feat, grad,
    fs_far, fr_far, fs_near, fr_near, ws, wr, ts, tr, sf, cs, cr,
    gs_far, gr_far, gs_near, gr_near, gs_z, gq,
    ssem, rsem,
):
    sec, dp = lax.axis_index("section"), lax.axis_index("dp")
    x, h = sec // 4, sec % 4
    l, y, c = dp // 8, (dp // 2) % 4, dp % 2
    z = 4 * h + l

    def dev(dx=0, dy=0, dz=0, flip=False):
        nx, ny, nz = (x + dx) % 4, (y + dy) % 4, (z + dz) % 16
        nc = 1 - c if flip else c
        return {"section": nx * 4 + nz // 4, "dp": (nz % 4) * 8 + ny * 2 + nc}

    copies = []

    def push(src, dst, where):
        i = len(copies)
        copy = pltpu.make_async_remote_copy(
            src_ref=src, dst_ref=dst, send_sem=ssem.at[i], recv_sem=rsem.at[i],
            device_id=where, device_id_type=MESH,
        )
        copy.start()
        copies.append(copy)
        return copy

    Z_WINDOW = (1, 15, 2)
    Z_CLASS = (4, 12, 8)
    barrier = pltpu.get_barrier_semaphore()
    partners = [dev(dz=k) for k in (1, 15, 2, 14, 4, 12, 8)]
    partners += [dev(dy=k) for k in (1, 2, 3)] + [dev(dx=k) for k in (1, 2, 3)] + [dev(flip=True)]
    for where in partners:
        pl.semaphore_signal(barrier, inc=1, device_id=where, device_id_type=MESH)
    pl.semaphore_wait(barrier, len(partners))

    hid_in = [push(hidden_ref.at[0], hid.at[h], dev(dz=k)) for k in Z_CLASS]
    mine = pl.ds(pl.multiple_of(c * 128, 128), 128)
    mine_a = pl.ds(pl.multiple_of(c * 128, 64), 64)
    mine_b = pl.ds(pl.multiple_of(c * 128 + 64, 64), 64)
    other = pl.ds(pl.multiple_of((1 - c) * 128, 128), 128)
    head_in = []
    for k in Z_CLASS:
        quarter = pl.multiple_of(((h + k // 4) % 4) * 128, 128)
        head_in.append(push(head_ref.at[pl.ds(quarter, 128)], heads.at[x, h, mine], dev(dz=k)))
    heads[x, h, mine] = head_ref[pl.ds(pl.multiple_of(h * 128, 128), 128), :]
    hid[h] = hidden_ref[0]

    from_left, from_right, core_in = [], [], []

    def spread(hh):
        block = heads.at[x, hh, mine]
        from_left.append(push(block, block, dev(dx=1)))
        from_right.append(push(block, block, dev(dx=-1)))
        core_in.append(push(block, block, dev(flip=True)))

    spread(h)

    lane = lax.broadcasted_iota(jnp.int32, (1, 128), 1)
    lane_y, lane_l, lane_h, lane_r = lane // 32, (lane // 8) % 4, (lane // 2) % 4, lane % 2
    row_of = lane_l * 16 + lane_y * 4 + lane_r
    target = jnp.zeros((1, 128), jnp.int32)
    for k in range(64):
        if (k // 2) % 2 == 0:
            target = jnp.where(row_of == k, targets_ref[k + 2 * c], target)
    weight = jnp.zeros((1, 128), F32)
    for k in range(4):
        weight = jnp.where(lane_h == k, nums_ref[x * 4 + k].astype(F32) / EXIT_DENOM, weight)

    for copy in hid_in:
        copy.wait_recv()
    gain = gain_ref[...]
    rows8 = jnp.concatenate([hid[k].astype(F32) for k in range(4)], axis=0)
    inverse = lax.rsqrt(jnp.mean(rows8 * rows8, axis=-1, keepdims=True) + EPSILON)
    hid8[...] = rows8
    inv8[...] = jnp.broadcast_to(inverse, (8, 128))
    n8[l] = (rows8 * inverse * gain).astype(BF16)
    window_in = [push(n8.at[l], n8.at[l], dev(dz=k)) for k in Z_WINDOW]

    def norm_rows(yy):
        return pl.ds(pl.multiple_of(c * 128 + yy * 32, 32), 32)

    for copy in window_in:
        copy.wait_recv()
    norm[norm_rows(y), :] = jnp.concatenate([n8[k].astype(F32) for k in range(4)], axis=0).astype(BF16)
    cols_a, cols_b = pl.ds(0, HALF), pl.ds(HALF, HALF)
    own_a, own_b = norm.at[norm_rows(y), cols_a], norm.at[norm_rows(y), cols_b]
    down_a = push(own_a, own_a, dev(dy=1))
    up_b = push(own_b, own_b, dev(dy=-1))
    down_b = push(own_b, own_b, dev(dy=1))
    up_a = push(own_a, own_a, dev(dy=-1))
    norm_core = [push(norm.at[norm_rows(y)], norm.at[norm_rows(y)], dev(flip=True))]

    order = [h] + [(h - k // 4) % 4 for k in Z_CLASS]
    for copy, hh in zip(head_in, order[1:]):
        copy.wait_recv()
        spread(hh)
    down_a.wait_recv()
    past = norm.at[norm_rows((y - 1) % 4), cols_a]
    far_a = push(past, past, dev(dy=1))
    up_b.wait_recv()
    past = norm.at[norm_rows((y + 1) % 4), cols_b]
    far_b = push(past, past, dev(dy=-1))
    far_head = []
    for k, hh in enumerate(order):
        from_left[k].wait_recv()
        part = heads.at[(x - 1) % 4, hh, mine_a]
        one = push(part, part, dev(dx=1))
        block = heads.at[(x - 1) % 4, hh, mine]
        core_in.append(push(block, block, dev(flip=True)))
        from_right[k].wait_recv()
        part = heads.at[(x + 1) % 4, hh, mine_b]
        two = push(part, part, dev(dx=-1))
        block = heads.at[(x + 1) % 4, hh, mine]
        core_in.append(push(block, block, dev(flip=True)))
        far_head.append((one, two))
    for pair, dy in (((down_b,), -1), ((up_a,), 1), ((far_a, far_b), 2)):
        for copy in pair:
            copy.wait_recv()
        block = norm.at[norm_rows((y + dy) % 4)]
        norm_core.append(push(block, block, dev(flip=True)))
    for (one, two), hh in zip(far_head, order):
        one.wait_recv()
        two.wait_recv()
        block = heads.at[(x + 2) % 4, hh, mine]
        core_in.append(push(block, block, dev(flip=True)))
    for copy in core_in:
        copy.wait_recv()

    tokens = pl.ds(pl.multiple_of(c * 128, 128), 128)
    logits[...] = jnp.zeros((256, 128), F32)

    def add_block(k, carry):
        cols = pl.ds(pl.multiple_of(k * 256, 256), 256)
        logits[...] += dot(heads[k // 4, k % 4], norm[tokens, cols], ((1,), (1,)))
        return carry

    lax.fori_loop(0, 16, add_block, 0)
    values = logits[...]
    peak = jnp.max(values, axis=0, keepdims=True)
    expo = jnp.exp(values - peak)
    total = jnp.sum(expo, axis=0, keepdims=True)
    first_peak = peak
    pad = jnp.zeros((6, 128), F32)
    stages = ([dev(dy=k) for k in (1, 3, 2)], [dev(dz=k) for k in Z_WINDOW], [dev(dz=k) for k in Z_CLASS])
    for stage, peers in enumerate(stages):
        stats[stage, 3] = jnp.concatenate([peak, total, pad], axis=0)
        arrivals = [push(stats.at[stage, 3], stats.at[stage, k], peer) for k, peer in enumerate(peers)]
        for copy in arrivals:
            copy.wait_recv()
        parts = [stats[stage, k] for k in range(4)]
        peak = functools.reduce(jnp.maximum, [part[0:1] for part in parts])
        total = sum(part[1:2] * jnp.exp(part[0:1] - peak) for part in parts)

    row = lax.broadcasted_iota(jnp.int32, (256, 128), 0)
    vocab_id = 512 * (2 * (l * 4 + y) + row // 128) + 128 * h + row % 128
    onehot = jnp.where(vocab_id == target, 1.0, 0.0)
    dlog = weight * (expo * (jnp.exp(first_peak - peak) / total) - onehot)
    dlog_t[...] = dlog.astype(BF16)
    dlog_in = push(dlog_t.at[other], dlog_2.at[c], dev(flip=True))
    dlog_2[c] = dlog_t[mine, :]
    dlog_n = dlog.T.astype(BF16)

    def feat_block(k, carry):
        cols = pl.ds(pl.multiple_of(k * 256, 256), 256)
        feat[:, cols] = dot(dlog_n, heads[k // 4, k % 4], ((1,), (0,)))
        return carry

    lax.fori_loop(0, 16, feat_block, 0)

    def feat_rows(dy):
        return pl.ds(pl.multiple_of(((y + dy) % 4) * 32, 32), 32)

    fs_far[0] = feat[feat_rows(2), cols_a].astype(BF16)
    fs_far[1] = feat[feat_rows(2), cols_b].astype(BF16)
    feat_far = [push(fs_far.at[0], fr_far.at[0], dev(dy=1)), push(fs_far.at[1], fr_far.at[1], dev(dy=-1))]
    fs_near[1] = feat[feat_rows(1), cols_b].astype(BF16)
    fs_near[2] = feat[feat_rows(-1), cols_a].astype(BF16)
    feat_near = [push(fs_near.at[1], fr_near.at[1], dev(dy=1)), push(fs_near.at[2], fr_near.at[2], dev(dy=-1))]

    dlog_in.wait_recv()
    for copy in norm_core:
        copy.wait_recv()
    dlog_all = jnp.concatenate([dlog_2[0], dlog_2[1]], axis=1)
    grad_order = [(h + k // 4) % 4 for k in (8, 4, 12, 0)]
    grad_far, grad_near = [], []
    for j, hh in enumerate(grad_order):
        def grad_block(k, carry, hh=hh):
            cols = pl.ds(pl.multiple_of((k * 4 + hh) * 256, 256), 256)
            grad[k, hh] = dot(dlog_all, norm[:, cols], ((1,), (0,)))
            return carry

        lax.fori_loop(0, 4, grad_block, 0)
        far = grad.at[(x + 2) % 4, hh]
        gs_far[j, 0] = far[0:64].astype(BF16)
        gs_far[j, 1] = far[64:128].astype(BF16)
        grad_far.append((
            push(gs_far.at[j, 0], gr_far.at[j, 0], dev(dx=1)),
            push(gs_far.at[j, 1], gr_far.at[j, 1], dev(dx=-1)),
        ))
        gs_near[j, 1] = grad.at[(x + 1) % 4, hh][64:128].astype(BF16)
        gs_near[j, 2] = grad.at[(x - 1) % 4, hh][0:64].astype(BF16)
        grad_near.append([
            push(gs_near.at[j, 1], gr_near.at[j, 1], dev(dx=1)),
            push(gs_near.at[j, 2], gr_near.at[j, 2], dev(dx=-1)),
        ])

    feat_far[0].wait_recv()
    fs_near[0] = (feat[feat_rows(1), cols_a] + fr_far[0].astype(F32)).astype(BF16)
    feat_near.append(push(fs_near.at[0], fr_near.at[0], dev(dy=1)))
    feat_far[1].wait_recv()
    fs_near[3] = (feat[feat_rows(-1), cols_b] + fr_far[1].astype(F32)).astype(BF16)
    feat_near.append(push(fs_near.at[3], fr_near.at[3], dev(dy=-1)))

    for j, hh in enumerate(grad_order):
        grad_far[j][0].wait_recv()
        gs_near[j, 0] = (grad.at[(x + 1) % 4, hh][0:64] + gr_far[j, 0].astype(F32)).astype(BF16)
        grad_near[j].append(push(gs_near.at[j, 0], gr_near.at[j, 0], dev(dx=1)))
        grad_far[j][1].wait_recv()
        gs_near[j, 3] = (grad.at[(x - 1) % 4, hh][64:128] + gr_far[j, 1].astype(F32)).astype(BF16)
        grad_near[j].append(push(gs_near.at[j, 3], gr_near.at[j, 3], dev(dx=-1)))

    for copy in feat_near:
        copy.wait_recv()
    near = [fr_near[k].astype(F32) for k in range(4)]
    summed = feat[feat_rows(0), :] + jnp.concatenate([near[0] + near[2], near[1] + near[3]], axis=1)
    feat[feat_rows(0), :] = summed
    for k in range(4):
        ws[k] = summed[8 * k : 8 * k + 8].astype(BF16)
    feat_window = [push(ws.at[(l + k) % 4], wr.at[i], dev(dz=k)) for i, k in enumerate(Z_WINDOW)]

    grad_z = []

    def finish_grad(j):
        hh = grad_order[j]
        for copy in grad_near[j]:
            copy.wait_recv()
        part = [gr_near[j, k].astype(F32) for k in range(4)]
        whole = grad[x, hh] + jnp.concatenate([part[0] + part[2], part[1] + part[3]], axis=0)
        if j == 3:
            gq[h] = whole.astype(BF16)
        else:
            gs_z[j] = whole.astype(BF16)
            grad_z.append(push(gs_z.at[j], gq.at[h], dev(dz=(8, 4, 12)[j])))

    finish_grad(0)
    finish_grad(1)
    for copy in feat_window:
        copy.wait_recv()
    own8 = pl.ds(pl.multiple_of(((y % 4) * 32) + l * 8, 8), 8)
    got = feat[own8, :] + wr[0].astype(F32) + wr[1].astype(F32) + wr[2].astype(F32)
    rows8 = hid8[...]
    inverse = inv8[:, 0:1]
    row_dots = jnp.mean(got * gain * rows8, axis=-1, keepdims=True)
    exits = inverse * (gain * got - rows8 * (inverse * inverse * row_dots))
    later = [None] * 4
    later[3] = exits[6:8]
    for k in (2, 1, 0):
        later[k] = exits[2 * k : 2 * k + 2] + later[k + 1]
    ts[...] = later[0].astype(BF16)
    planes = [push(ts, tr.at[i], dev(dx=k)) for i, k in enumerate((1, 2, 3))]
    finish_grad(2)
    finish_grad(3)
    above = jnp.zeros((2, D), F32)
    for i, k in enumerate((1, 2, 3)):
        planes[i].wait_recv()
        above += jnp.where(x + (4 - k) < 4, 1.0, 0.0) * tr[i].astype(F32)
    for k in range(4):
        value = later[k] + above
        sf[k] = value
        cs[k] = value.astype(BF16)
    last = [push(cs.at[(h + k // 4) % 4], cr.at[i], dev(dz=k)) for i, k in enumerate(Z_CLASS)]
    for copy in last:
        copy.wait_recv()
    result = sf[h] + top_ref[...].astype(F32)
    for i in range(3):
        result += cr[i].astype(F32)
    ghid_ref[0] = result.astype(BF16)
    for copy in grad_z:
        copy.wait_recv()
    for k in range(4):
        ghead_ref[k * 128 : k * 128 + 128, :] = gq[k]
    for copy in copies:
        copy.wait_send()


def body(hidden, norm_gain, exit_head, targets, loss_numerators, top_grad):
    vmem = pl.BlockSpec(memory_space=pltpu.VMEM)
    smem = pl.BlockSpec(memory_space=pltpu.SMEM)
    return pl.pallas_call(
        kernel,
        out_shape=(
            jax.ShapeDtypeStruct(exit_head.shape, BF16),
            jax.ShapeDtypeStruct(hidden.shape, BF16),
        ),
        in_specs=[vmem, vmem, vmem, smem, smem, vmem],
        out_specs=(vmem, vmem),
        scratch_shapes=[
            pltpu.VMEM((4, 2, D), BF16),
            pltpu.VMEM((8, D), F32),
            pltpu.VMEM((8, 128), F32),
            pltpu.VMEM((4, 8, D), BF16),
            pltpu.VMEM((256, D), BF16),
            pltpu.VMEM((4, 4, 256, 256), BF16),
            pltpu.VMEM((256, 128), F32),
            pltpu.VMEM((3, 4, 8, 128), F32),
            pltpu.VMEM((256, 128), BF16),
            pltpu.VMEM((2, 128, 128), BF16),
            pltpu.VMEM((128, D), F32),
            pltpu.VMEM((4, 4, 128, 256), F32),
            pltpu.VMEM((2, 32, HALF), BF16),
            pltpu.VMEM((2, 32, HALF), BF16),
            pltpu.VMEM((4, 32, HALF), BF16),
            pltpu.VMEM((4, 32, HALF), BF16),
            pltpu.VMEM((4, 8, D), BF16),
            pltpu.VMEM((3, 8, D), BF16),
            pltpu.VMEM((2, D), BF16),
            pltpu.VMEM((3, 2, D), BF16),
            pltpu.VMEM((4, 2, D), F32),
            pltpu.VMEM((4, 2, D), BF16),
            pltpu.VMEM((3, 2, D), BF16),
            pltpu.VMEM((4, 2, 64, 256), BF16),
            pltpu.VMEM((4, 2, 64, 256), BF16),
            pltpu.VMEM((4, 4, 64, 256), BF16),
            pltpu.VMEM((4, 4, 64, 256), BF16),
            pltpu.VMEM((3, 128, 256), BF16),
            pltpu.VMEM((4, 128, 256), BF16),
            pltpu.SemaphoreType.DMA((COPIES,)),
            pltpu.SemaphoreType.DMA((COPIES,)),
        ],
        compiler_params=pltpu.CompilerParams(
            collective_id=0, has_side_effects=True, vmem_limit_bytes=40 * 1024 * 1024
        ),
        name="exit_head_backward",
    )(hidden, norm_gain.reshape(1, D), exit_head, targets, loss_numerators, top_grad)


def solution(mesh):
    placed = (P("section", "dp", None), P(), P("dp", "section"), P(), P(), P("dp", None))
    return jax.shard_map(
        body,
        mesh=mesh,
        in_specs=placed,
        out_specs=(P("dp", "section"), P("section", "dp", None)),
        check_vma=False,
    )
```

```python
import functools

import jax
import jax.numpy as jnp
from jax import lax
from jax.experimental import pallas as pl
from jax.experimental.pallas import tpu as pltpu
from jax.sharding import PartitionSpec as P

MESH = pl.DeviceIdType.MESH
EXIT_DENOM = 16
EPSILON = 1e-05
F32 = jnp.float32
BF16 = jnp.bfloat16
D = 4096
SENDS = 18
RECVS = 36
LOCALS = 6
Z_WINDOW = (1, 15, 2)
Z_CLASS = (8, 4, 12)
RING = (1, 3, 2)


def dot(a, b, contract):
    return lax.dot_general(a, b, (contract, ((), ())), preferred_element_type=F32)


def kernel(
    hidden_ref, gain_ref, head_ref, targets_ref, nums_ref, top_ref,
    ghead_ref, ghid_ref,
    hid, gain_v, top_v, hid8, inv8, pieces, norm, heads, logits, stats_1, stats_2, dlog_t, dlog_2,
    coef, hs, hr, hx, feat, fs, fr, wo, ws, wr, ts, tr, sf, cs, cr, grad, gs, gr, gs_z, gq,
    targets_s, nums_s, send_sem, recv_sem, local_sem,
):
    sec, dp = lax.axis_index("section"), lax.axis_index("dp")
    x, h = sec // 4, sec % 4
    l, y, c = dp // 8, (dp // 2) % 4, dp % 2
    z = 4 * h + l

    def dev(dx=0, dy=0, dz=0, flip=False):
        nx, ny, nz = (x + dx) % 4, (y + dy) % 4, (z + dz) % 16
        nc = 1 - c if flip else c
        return {"section": nx * 4 + nz // 4, "dp": (nz % 4) * 8 + ny * 2 + nc}

    counts = {"send": 0, "recv": 0}
    sent = []

    def new_recv():
        counts["recv"] += 1
        return recv_sem.at[counts["recv"] - 1]

    def new_send(total):
        counts["send"] += 1
        sem = send_sem.at[counts["send"] - 1]
        sent.append((sem, total))
        return sem

    def push(src, dst, where, s_sem, r_sem):
        pltpu.make_async_remote_copy(
            src_ref=src, dst_ref=dst, send_sem=s_sem, recv_sem=r_sem,
            device_id=where, device_id_type=MESH,
        ).start()

    def wait(sem, total):
        pltpu.make_async_copy(total, total, sem).wait()

    mine = pl.ds(pl.multiple_of(c * 128, 128), 128)
    other = pl.ds(pl.multiple_of((1 - c) * 128, 128), 128)

    def quarter(hh):
        return head_ref.at[pl.ds(pl.multiple_of(hh * 128, 128), 128)]

    locals_ = [
        pltpu.make_async_copy(src, dst, local_sem.at[i])
        for i, (src, dst) in enumerate((
            (hidden_ref.at[0], hid.at[h]),
            (quarter(h), heads.at[x, h, mine]),
            (gain_ref, gain_v),
            (targets_ref, targets_s),
            (nums_ref, nums_s),
            (top_ref, top_v),
        ))
    ]
    for copy in locals_:
        copy.start()

    barrier = pltpu.get_barrier_semaphore()
    near_z = (1, 15, 2, 14)
    partners = [dev(dz=k) for k in Z_CLASS + near_z] + [dev(dx=k) for k in RING] + [dev(flip=True)]
    partners += [dev(dy=k) for k in RING] + [dev(dy=i, dz=k) for i in RING for k in near_z]
    for where in partners:
        pl.semaphore_signal(barrier, inc=1, device_id=where, device_id_type=MESH)
    pl.semaphore_wait(barrier, len(partners))

    hid_s, hid_r = new_send(hid.at[0:3]), new_recv()
    for k in Z_CLASS:
        push(hidden_ref.at[0], hid.at[h], dev(dz=k), hid_s, hid_r)
    headz_s, headz_r = new_send(heads.at[0, 0:3, 0:128]), [new_recv() for _ in Z_CLASS]

    def transpose(which):
        for i in which:
            k = Z_CLASS[i]
            push(quarter((h + k // 4) % 4), heads.at[x, h, mine], dev(dz=k), headz_s, headz_r[i])

    transpose((0,))
    headx_s, headx_r = new_send(heads.at[0:3, :, 0:128]), [new_recv() for _ in range(4)]

    def spread(hh, sem):
        block = heads.at[x, hh, mine]
        for k in RING:
            push(block, block, dev(dx=k), headx_s, sem)

    locals_[1].wait()
    spread(h, headx_r[0])
    for i in (0, 2, 3, 4, 5):
        locals_[i].wait()

    lane = lax.broadcasted_iota(jnp.int32, (1, 128), 1)
    lane_y, lane_l, lane_h, lane_r = lane // 32, (lane // 8) % 4, (lane // 2) % 4, lane % 2
    row_of = lane_l * 16 + lane_y * 4 + lane_r
    target = jnp.zeros((1, 128), jnp.int32)
    for k in range(64):
        if (k // 2) % 2 == 0:
            target = jnp.where(row_of == k, targets_s[k + 2 * c], target)
    weight = jnp.zeros((1, 128), F32)
    for k in range(4):
        weight = jnp.where(lane_h == k, nums_s[x * 4 + k].astype(F32) / EXIT_DENOM, weight)

    slot = lax.broadcasted_iota(jnp.int32, (32, 1), 0)
    target_col = jnp.zeros((32, 1), jnp.int32)
    for k in range(32):
        target_col = jnp.where(slot == k, targets_s[(k // 2) % 4 * 16 + k // 8 * 4 + k % 2 + 2 * c], target_col)
    first_id = 1024 * (l * 4 + y) + 128 * h
    lane_id = lax.broadcasted_iota(jnp.int32, (1, 256), 1)
    picks = jnp.where(first_id + lane_id + 384 * (lane_id // 128) == target_col, 1.0, 0.0).astype(BF16)

    wait(hid_r, hid.at[0:3])
    gain = gain_v[...]
    rows8 = jnp.concatenate([hid[k].astype(F32) for k in range(4)], axis=0)
    inverse = lax.rsqrt(jnp.mean(rows8 * rows8, axis=-1, keepdims=True) + EPSILON)
    pieces[y, l] = (rows8 * inverse * gain).astype(BF16)
    window_s, window_r = new_send(pieces.at[0, 0:3]), [new_recv() for _ in Z_WINDOW]
    ring_s, ring_r = new_send(pieces.at[0:3]), [new_recv() for _ in RING]
    own = pieces.at[y, l]
    for k, sem in zip((1, 15), window_r):
        push(own, own, dev(dz=k), window_s, sem)
    for k, cols in ((2, pl.ds(0, D // 2)), (14, pl.ds(D // 2, D // 2))):
        part = pieces.at[y, l, :, cols]
        push(part, part, dev(dz=k), window_s, window_r[2])
    transpose((1, 2))
    for k, sem in zip(RING, ring_r):
        push(own, own, dev(dy=k), ring_s, sem)
    hid8[...] = rows8
    inv8[...] = jnp.broadcast_to(inverse, (8, 128))

    for k, sem in zip(Z_WINDOW, window_r):
        piece = pieces.at[y, (l - k) % 4]
        wait(sem, piece)
        for kk, ring in zip(RING, ring_r):
            push(piece, piece, dev(dy=kk), ring_s, ring)

    order = [h] + [(h - k // 4) % 4 for k in Z_CLASS[1:] + Z_CLASS[:1]]
    for j in (1, 2, 3):
        wait(headz_r[j % 3], heads.at[x, order[j], mine])
        spread(order[j], headx_r[j])

    def assemble(yy):
        for half in range(2):
            both = jnp.concatenate([pieces[yy, 2 * half + k].astype(F32) for k in range(2)], axis=0)
            rows = pl.ds(pl.multiple_of(c * 128 + yy * 32 + half * 16, 16), 16)
            norm[rows, :] = both.astype(BF16)

    assemble(y)
    for k, sem in zip(RING, ring_r):
        wait(sem, pieces.at[0])
        assemble((y - k) % 4)
    norm_s, norm_r = new_send(norm.at[mine]), new_recv()
    push(norm.at[mine], norm.at[mine], dev(flip=True), norm_s, norm_r)

    core_s, core_r = new_send(heads.at[:, :, 0:128]), [new_recv() for _ in range(4)]
    logits[...] = jnp.zeros((256, 128), F32)
    for j, hh in enumerate(order):
        wait(headx_r[j], heads.at[0:3, hh, mine])
        block = heads.at[:, hh, mine]
        push(block, block, dev(flip=True), core_s, core_r[j])
        wait(core_r[j], block)
        part = jnp.zeros((256, 128), F32)
        for k in range(4):
            cols = pl.ds(pl.multiple_of((k * 4 + hh) * 256, 256), 256)
            part += dot(heads[k, hh], norm[mine, cols], ((1,), (1,)))
        logits[...] += part
    values = logits[...]
    row = lax.broadcasted_iota(jnp.int32, (256, 128), 0)
    at_target = first_id + row + 384 * (row // 128) == target
    first_peak = jnp.max(values, axis=0, keepdims=True)
    expo = jnp.exp(values - first_peak)
    others = jnp.where(at_target, 0.0, expo)
    own_stats = jnp.concatenate(
        [
            first_peak,
            jnp.sum(others, axis=0, keepdims=True),
            jnp.sum(jnp.where(at_target, expo, 0.0), axis=0, keepdims=True),
            jnp.zeros((5, 128), F32),
        ],
        axis=0,
    )

    def send_stats(stats, mine_now, peers):
        n = len(peers)
        s_sem, r_sem = new_send(stats.at[0:n]), new_recv()
        stats[n] = mine_now
        for i, where in enumerate(peers):
            push(stats.at[n], stats.at[i], where, s_sem, r_sem)
        return r_sem

    def combine(stats, r_sem, n):
        wait(r_sem, stats.at[0:n])
        parts = [stats[i] for i in range(n + 1)]
        top = functools.reduce(jnp.maximum, [part[0:1] for part in parts])
        sums = sum(part[1:3] * jnp.exp(part[0:1] - top) for part in parts)
        return jnp.concatenate([top, sums, jnp.zeros((5, 128), F32)], axis=0)

    peers = [dev(dy=i, dz=k) for k in Z_WINDOW + (0,) for i in RING + (0,)][:-1]
    stats_r = send_stats(stats_1, own_stats, peers)

    pick_s, pick_r = new_send(hr), new_recv()
    for k in range(4):
        part = dot(picks, heads[x, k], ((1,), (0,)))
        for yy in range(4):
            hs[yy, :, 256 * k : 256 * k + 256] = part[8 * yy : 8 * yy + 8].astype(BF16)
    for i, k in enumerate(RING):
        push(hs.at[(y + k) % 4], hr.at[i], dev(dy=k), pick_s, pick_r)

    others_n = others.T.astype(BF16)
    feat_s, feat_r = new_send(fr), [new_recv() for _ in range(4)]
    for q in range(4):
        for k in range(4):
            part = dot(others_n, heads[q, k], ((1,), (0,)))
            for yy in range(4):
                rows = part[32 * yy : 32 * yy + 32]
                feat[q, yy, :, 256 * k : 256 * k + 256] = rows
                fs[q, yy, :, 256 * k : 256 * k + 256] = rows.astype(BF16)
        for i, k in enumerate(RING):
            push(fs.at[q, (y + k) % 4], fr.at[q, i], dev(dy=k), feat_s, feat_r[q])

    summed_stats = combine(stats_1, stats_r, 15)
    stats_r = send_stats(stats_2, summed_stats, [dev(dz=k) for k in Z_CLASS])
    wait(pick_r, hr)
    hx[x] = (hs[y].astype(F32) + hr[0].astype(F32) + hr[1].astype(F32) + hr[2].astype(F32)).astype(BF16)
    pickx_s, pickx_r = new_send(hx.at[0:3]), new_recv()
    for k in RING:
        push(hx.at[x], hx.at[x], dev(dx=k), pickx_s, pickx_r)
    summed_stats = combine(stats_2, stats_r, 3)
    peak = summed_stats[0:1]
    total = summed_stats[1:2] + summed_stats[2:3]
    scale = weight / total

    dlog = expo * (scale * jnp.exp(first_peak - peak)) - jnp.where(at_target, weight, 0.0)
    dlog_t[...] = dlog.astype(BF16)
    dlog_s, dlog_r = new_send(dlog_2.at[0]), new_recv()
    push(dlog_t.at[other], dlog_2.at[c], dev(flip=True), dlog_s, dlog_r)
    dlog_2[c] = dlog_t[mine, :]
    coef[...] = jnp.concatenate(
        [scale * jnp.exp(stats_1[i][0:1] - peak) for i in (12, 13, 14, 15)]
        + [scale * summed_stats[1:2], jnp.zeros((123, 128), F32)],
        axis=0,
    ).T
    factors = coef[pl.ds(pl.multiple_of(32 * y, 32), 32), :]

    wait(dlog_r, dlog_2.at[0])
    wait(norm_r, norm.at[other])
    dlog_all = jnp.concatenate([dlog_2[0], dlog_2[1]], axis=1)
    grad_order = [(h + k // 4) % 4 for k in Z_CLASS] + [h]
    grad_s, grad_r = new_send(gr), [new_recv() for _ in range(4)]

    def start_grad(j):
        for k in range(4):
            cols = pl.ds(pl.multiple_of((k * 4 + grad_order[j]) * 256, 256), 256)
            part = dot(dlog_all, norm[:, cols], ((1,), (0,)))
            grad[j, k] = part
            gs[j, k] = part.astype(BF16)
        for i, k in enumerate(RING):
            push(gs.at[j, (x + k) % 4], gr.at[j, i], dev(dx=k), grad_s, grad_r[j])

    swin_s, swin_r = new_send(wr), new_recv()
    gradz_s, gradz_r = new_send(gs_z), new_recv()

    def finish_feat(q):
        wait(feat_r[q], fr.at[q])
        summed = factors[:, 3:4] * feat[q, y]
        for i in range(3):
            summed += factors[:, i : i + 1] * fr[q, i].astype(F32)
        rows = hx[q].astype(F32)
        rows = jnp.concatenate([rows[2 * (k // 4) : 2 * (k // 4) + 2] for k in range(16)], axis=0)
        summed -= factors[:, 4:5] * rows
        for k in range(4):
            wo[q, k] = summed[8 * k : 8 * k + 8]
            ws[q, k] = summed[8 * k : 8 * k + 8].astype(BF16)
        for i, k in enumerate((1, 15, 2 if q < 2 else 14)):
            push(ws.at[q, (l + k) % 4], wr.at[q, i], dev(dz=k), swin_s, swin_r)

    def finish_grad(j):
        wait(grad_r[j], gr.at[j])
        whole = grad[j, x] + gr[j, 0].astype(F32) + gr[j, 1].astype(F32) + gr[j, 2].astype(F32)
        if j == 3:
            gq[h] = whole.astype(BF16)
        else:
            gs_z[j] = whole.astype(BF16)
            push(gs_z.at[j], gq.at[h], dev(dz=Z_CLASS[j]), gradz_s, gradz_r)

    start_grad(0)
    wait(pickx_r, hx.at[0:3])
    finish_feat(0)
    finish_feat(1)
    start_grad(1)
    finish_feat(2)
    finish_feat(3)
    start_grad(2)
    start_grad(3)
    for j in range(4):
        finish_grad(j)

    wait(swin_r, wr)
    got = jnp.concatenate(
        [wo[q, l] + wr[q, 0].astype(F32) + wr[q, 1].astype(F32) + wr[q, 2].astype(F32) for q in range(4)],
        axis=1,
    )
    rows8 = hid8[...]
    inverse = inv8[:, 0:1]
    row_dots = jnp.mean(got * gain * rows8, axis=-1, keepdims=True)
    exits = inverse * (gain * got - rows8 * (inverse * inverse * row_dots))
    later = [None] * 4
    later[3] = exits[6:8]
    for k in (2, 1, 0):
        later[k] = exits[2 * k : 2 * k + 2] + later[k + 1]
    ts[...] = later[0].astype(BF16)
    plane_s, plane_r = new_send(tr), new_recv()
    for i, k in enumerate(RING):
        push(ts, tr.at[i], dev(dx=k), plane_s, plane_r)
    wait(plane_r, tr)
    above = jnp.zeros((2, D), F32)
    for i, k in enumerate(RING):
        above += jnp.where(x + (4 - k) < 4, 1.0, 0.0) * tr[i].astype(F32)
    for k in range(4):
        value = later[k] + above
        sf[k] = value
        cs[k] = value.astype(BF16)
    class_s, class_r = new_send(cr), new_recv()
    for i, k in enumerate(Z_CLASS):
        push(cs.at[(h + k // 4) % 4], cr.at[i], dev(dz=k), class_s, class_r)
    wait(class_r, cr)
    result = sf[h] + top_v[...].astype(F32)
    for i in range(3):
        result += cr[i].astype(F32)
    ghid_ref[0] = result.astype(BF16)
    wait(gradz_r, gq.at[0:3])
    for k in range(4):
        ghead_ref[k * 128 : k * 128 + 128, :] = gq[k]
    assert counts == {"send": SENDS, "recv": RECVS}
    for sem, ref in sent:
        wait(sem, ref)


def body(hidden, norm_gain, exit_head, targets, loss_numerators, top_grad):
    vmem = pl.BlockSpec(memory_space=pltpu.VMEM)
    where_it_is = pl.BlockSpec(memory_space=pl.ANY)
    return pl.pallas_call(
        kernel,
        out_shape=(
            jax.ShapeDtypeStruct(exit_head.shape, BF16),
            jax.ShapeDtypeStruct(hidden.shape, BF16),
        ),
        in_specs=[where_it_is] * 6,
        out_specs=(vmem, vmem),
        scratch_shapes=[
            pltpu.VMEM((4, 2, D), BF16),
            pltpu.VMEM((1, D), F32),
            pltpu.VMEM((2, D), BF16),
            pltpu.VMEM((8, D), F32),
            pltpu.VMEM((8, 128), F32),
            pltpu.VMEM((4, 4, 8, D), BF16),
            pltpu.VMEM((256, D), BF16),
            pltpu.VMEM((4, 4, 256, 256), BF16),
            pltpu.VMEM((256, 128), F32),
            pltpu.VMEM((16, 8, 128), F32),
            pltpu.VMEM((4, 8, 128), F32),
            pltpu.VMEM((256, 128), BF16),
            pltpu.VMEM((2, 128, 128), BF16),
            pltpu.VMEM((128, 128), F32),
            pltpu.VMEM((4, 8, 1024), BF16),
            pltpu.VMEM((3, 8, 1024), BF16),
            pltpu.VMEM((4, 8, 1024), BF16),
            pltpu.VMEM((4, 4, 32, 1024), F32),
            pltpu.VMEM((4, 4, 32, 1024), BF16),
            pltpu.VMEM((4, 3, 32, 1024), BF16),
            pltpu.VMEM((4, 4, 8, 1024), F32),
            pltpu.VMEM((4, 4, 8, 1024), BF16),
            pltpu.VMEM((4, 3, 8, 1024), BF16),
            pltpu.VMEM((2, D), BF16),
            pltpu.VMEM((3, 2, D), BF16),
            pltpu.VMEM((4, 2, D), F32),
            pltpu.VMEM((4, 2, D), BF16),
            pltpu.VMEM((3, 2, D), BF16),
            pltpu.VMEM((4, 4, 128, 256), F32),
            pltpu.VMEM((4, 4, 128, 256), BF16),
            pltpu.VMEM((4, 3, 128, 256), BF16),
            pltpu.VMEM((3, 128, 256), BF16),
            pltpu.VMEM((4, 128, 256), BF16),
            pltpu.SMEM((64,), jnp.int32),
            pltpu.SMEM((16,), jnp.int32),
            pltpu.SemaphoreType.DMA((SENDS,)),
            pltpu.SemaphoreType.DMA((RECVS,)),
            pltpu.SemaphoreType.DMA((LOCALS,)),
        ],
        compiler_params=pltpu.CompilerParams(
            collective_id=0, has_side_effects=True, vmem_limit_bytes=60 * 1024 * 1024
        ),
        name="exit_head_backward",
    )(hidden, norm_gain.reshape(1, D), exit_head, targets, loss_numerators, top_grad)


def solution(mesh):
    placed = (P("section", "dp", None), P(), P("dp", "section"), P(), P(), P("dp", None))
    return jax.shard_map(
        body,
        mesh=mesh,
        in_specs=placed,
        out_specs=(P("dp", "section"), P("section", "dp", None)),
        check_vma=False,
    )
```

```python
import functools

import jax
import jax.numpy as jnp
from jax import lax
from jax.experimental import pallas as pl
from jax.experimental.pallas import tpu as pltpu
from jax.sharding import PartitionSpec as P

MESH = pl.DeviceIdType.MESH
EXIT_DENOM = 16
EPSILON = 1e-05
F32 = jnp.float32
BF16 = jnp.bfloat16
D = 4096
SENDS = 24
RECVS = 55
LOCALS = 6
Z_WINDOW = (1, 15, 2)
Z_CLASS = (8, 4, 12)
RING = (1, 3, 2)


def dot(a, b, contract):
    return lax.dot_general(a, b, (contract, ((), ())), preferred_element_type=F32)


def kernel(
    hidden_ref, gain_ref, head_ref, targets_ref, nums_ref, top_ref,
    ghead_ref, ghid_ref,
    raw, gain_v, top_v, norm, heads, logits, stats_1, stats_2, expo_t, expo_all, own_all, plane_all, norm_all,
    coef, hs, hr, hx, feat, fs, fr, wo, ws, wr, ts, tr, sf, cs, cr,
    targets_s, nums_s, send_sem, recv_sem, local_sem,
):
    sec, dp = lax.axis_index("section"), lax.axis_index("dp")
    x, h = sec // 4, sec % 4
    l, y, c = dp // 8, (dp // 2) % 4, dp % 2
    z = 4 * h + l

    def dev(dx=0, dy=0, dz=0, flip=False):
        nx, ny, nz = (x + dx) % 4, (y + dy) % 4, (z + dz) % 16
        nc = 1 - c if flip else c
        return {"section": nx * 4 + nz // 4, "dp": (nz % 4) * 8 + ny * 2 + nc}

    counts = {"send": 0, "recv": 0}
    sent = []

    def new_recv():
        counts["recv"] += 1
        return recv_sem.at[counts["recv"] - 1]

    def new_send(total):
        counts["send"] += 1
        sem = send_sem.at[counts["send"] - 1]
        sent.append((sem, total))
        return sem

    def push(src, dst, where, s_sem, r_sem):
        pltpu.make_async_remote_copy(
            src_ref=src, dst_ref=dst, send_sem=s_sem, recv_sem=r_sem,
            device_id=where, device_id_type=MESH,
        ).start()

    def wait(sem, total):
        pltpu.make_async_copy(total, total, sem).wait()

    mine = pl.ds(pl.multiple_of(c * 128, 128), 128)
    other = pl.ds(pl.multiple_of((1 - c) * 128, 128), 128)

    def quarter(hh):
        return head_ref.at[pl.ds(pl.multiple_of(hh * 128, 128), 128)]

    locals_ = [
        pltpu.make_async_copy(src, dst, local_sem.at[i])
        for i, (src, dst) in enumerate((
            (hidden_ref.at[0], raw.at[y, l, h]),
            (quarter(h), heads.at[x, h, mine]),
            (gain_ref, gain_v),
            (targets_ref, targets_s),
            (nums_ref, nums_s),
            (top_ref, top_v),
        ))
    ]
    for copy in locals_:
        copy.start()

    barrier = pltpu.get_barrier_semaphore()
    near_z = (1, 15, 2, 14)
    partners = [dev(dz=k) for k in Z_CLASS + near_z] + [dev(dx=k) for k in RING] + [dev(flip=True)]
    partners += [dev(dy=k) for k in RING] + [dev(dy=i, dz=k) for i in RING for k in near_z]
    for where in partners:
        pl.semaphore_signal(barrier, inc=1, device_id=where, device_id_type=MESH)
    pl.semaphore_wait(barrier, len(partners))

    class_pieces = [new_recv() for _ in Z_CLASS]
    window_pieces = [[new_recv() for _ in range(3)] for _ in range(4)]
    ring_pieces = [new_recv() for _ in RING]
    classp_s, windowp_s, ringp_s = new_send(raw.at[0, 0, 0:3]), new_send(raw.at[0, 0:3]), new_send(raw.at[0:3])
    cols_a, cols_b = pl.ds(0, D // 2), pl.ds(D // 2, D // 2)
    mine_now = hidden_ref.at[0]
    for k, sem in zip(Z_CLASS, class_pieces):
        push(mine_now, raw.at[y, l, h], dev(dz=k), classp_s, sem)

    def to_window(src, slot, sems):
        push(src, slot, dev(dz=1), windowp_s, sems[0])
        push(src, slot, dev(dz=15), windowp_s, sems[1])
        push(src.at[:, cols_a], slot.at[:, cols_a], dev(dz=2), windowp_s, sems[2])
        push(src.at[:, cols_b], slot.at[:, cols_b], dev(dz=14), windowp_s, sems[2])

    def to_ring(src, slot):
        for k, sem in zip(RING, ring_pieces):
            push(src, slot, dev(dy=k), ringp_s, sem)

    to_window(mine_now, raw.at[y, l, h], window_pieces[0])
    to_ring(mine_now, raw.at[y, l, h])
    headz_s, headz_r = new_send(heads.at[0, 0:3, 0:128]), [new_recv() for _ in Z_CLASS]

    def transpose(which):
        for i in which:
            k = Z_CLASS[i]
            push(quarter((h + k // 4) % 4), heads.at[x, h, mine], dev(dz=k), headz_s, headz_r[i])

    transpose((1, 2))
    headx_s, headx_r = new_send(heads.at[0:3, :, 0:128]), [new_recv() for _ in range(4)]

    def spread(hh, sem):
        block = heads.at[x, hh, mine]
        for k in RING:
            push(block, block, dev(dx=k), headx_s, sem)

    locals_[1].wait()
    spread(h, headx_r[0])
    for i in (0, 2, 3, 4, 5):
        locals_[i].wait()

    lane = lax.broadcasted_iota(jnp.int32, (1, 128), 1)
    lane_y, lane_l, lane_h, lane_r = lane // 32, (lane // 8) % 4, (lane // 2) % 4, lane % 2
    row_of = lane_l * 16 + lane_y * 4 + lane_r
    def lane_targets(core):
        found = jnp.zeros((1, 128), jnp.int32)
        for k in range(64):
            if (k // 2) % 2 == 0:
                found = jnp.where(row_of == k, targets_s[k + 2 * core], found)
        return found

    def lane_weights(plane):
        found = jnp.zeros((1, 128), F32)
        for k in range(4):
            found = jnp.where(lane_h == k, nums_s[plane * 4 + k].astype(F32) / EXIT_DENOM, found)
        return found

    target, weight = lane_targets(c), lane_weights(x)
    both_targets = jnp.concatenate([lane_targets(0), lane_targets(1)], axis=1)
    slot = lax.broadcasted_iota(jnp.int32, (32, 1), 0)
    target_col = jnp.zeros((32, 1), jnp.int32)
    for k in range(32):
        target_col = jnp.where(slot == k, targets_s[(k // 2) % 4 * 16 + k // 8 * 4 + k % 2 + 2 * c], target_col)
    first_id = 1024 * (l * 4 + y) + 128 * h
    lane_id = lax.broadcasted_iota(jnp.int32, (1, 256), 1)
    picks = jnp.where(first_id + lane_id + 384 * (lane_id // 128) == target_col, 1.0, 0.0).astype(BF16)

    def from_window(i, steps):
        for n, k in enumerate((1, 15)):
            slot = raw.at[y, (l - k) % 4, (((z - k) % 16) // 4 - steps) % 4]
            wait(window_pieces[i][n], slot)
            to_ring(slot, slot)

    def from_far(i, steps):
        wait(window_pieces[i][2], raw.at[0, 0, 0])
        for k, cols in ((2, cols_a), (14, cols_b)):
            slot = raw.at[y, (l + 2) % 4, (((z - k) % 16) // 4 - steps) % 4, :, cols]
            for kk, sem in zip(RING, ring_pieces):
                push(slot, slot, dev(dy=kk), ringp_s, sem)

    def from_class(i, steps):
        slot = raw.at[y, l, (h - steps) % 4]
        wait(class_pieces[i], slot)
        to_window(slot, slot, window_pieces[i + 1])
        to_ring(slot, slot)

    order = [h] + [(h - k // 4) % 4 for k in Z_CLASS[1:] + Z_CLASS[:1]]

    def from_head(j):
        wait(headz_r[j % 3], heads.at[x, order[j], mine])
        spread(order[j], headx_r[j])

    from_window(0, 0)
    from_far(0, 0)
    from_class(1, 1)
    from_class(2, 3)
    transpose((0,))
    from_class(0, 2)
    from_head(1)
    from_head(2)
    from_window(2, 1)
    from_window(3, 3)
    from_far(2, 1)
    from_far(3, 3)
    from_window(1, 2)
    from_far(1, 2)
    gain = gain_v[...]

    def rows_of(yy, ll):
        rows = jnp.concatenate([raw[yy, ll, k].astype(F32) for k in range(4)], axis=0)
        return rows, lax.rsqrt(jnp.mean(rows * rows, axis=-1, keepdims=True) + EPSILON)

    def assemble(yy):
        for half in range(2):
            both = []
            for ll in (2 * half, 2 * half + 1):
                rows, inverse = rows_of(yy, ll)
                both.append(rows * inverse * gain)
            at = pl.ds(pl.multiple_of(yy * 32 + half * 16, 16), 16)
            norm[at, :] = jnp.concatenate(both, axis=0).astype(BF16)

    assemble(y)
    from_head(3)
    for k, sem in zip(RING, ring_pieces):
        wait(sem, raw.at[0])
        assemble((y - k) % 4)

    core_s, core_r = new_send(heads.at[:, :, 0:128]), [new_recv() for _ in range(4)]
    logits[...] = jnp.zeros((256, 128), F32)
    for j, hh in enumerate(order):
        wait(headx_r[j], heads.at[0:3, hh, mine])
        block = heads.at[:, hh, mine]
        push(block, block, dev(flip=True), core_s, core_r[j])
        wait(core_r[j], block)
        part = jnp.zeros((256, 128), F32)
        for k in range(4):
            cols = pl.ds(pl.multiple_of((k * 4 + hh) * 256, 256), 256)
            part += dot(heads[k, hh], norm[:, cols], ((1,), (1,)))
        logits[...] += part
    values = logits[...]
    row = lax.broadcasted_iota(jnp.int32, (256, 128), 0)
    at_target = first_id + row + 384 * (row // 128) == target
    first_peak = jnp.max(values, axis=0, keepdims=True)
    expo = jnp.exp(values - first_peak)
    others = jnp.where(at_target, 0.0, expo)
    own_stats = jnp.concatenate(
        [
            first_peak,
            jnp.sum(others, axis=0, keepdims=True),
            jnp.sum(jnp.where(at_target, expo, 0.0), axis=0, keepdims=True),
            jnp.zeros((5, 128), F32),
        ],
        axis=0,
    )

    def send_stats(stats, mine_now, peers):
        n = len(peers)
        s_sem, r_sem = new_send(stats.at[0:n]), new_recv()
        stats[n] = mine_now
        for i, where in enumerate(peers):
            push(stats.at[n], stats.at[i], where, s_sem, r_sem)
        return r_sem

    def combine(stats, r_sem, n):
        wait(r_sem, stats.at[0:n])
        parts = [stats[i] for i in range(n + 1)]
        top = functools.reduce(jnp.maximum, [part[0:1] for part in parts])
        sums = sum(part[1:3] * jnp.exp(part[0:1] - top) for part in parts)
        return jnp.concatenate([top, sums, jnp.zeros((5, 128), F32)], axis=0)

    peers = [dev(dy=i, dz=k) for k in Z_WINDOW + (0,) for i in RING + (0,)][:-1]
    stats_r = send_stats(stats_1, own_stats, peers)

    expo_t[...] = others.astype(BF16)
    core_e_s, core_e_r = new_send(expo_all.at[0, 0, 0]), new_recv()
    push(expo_t.at[other], expo_all.at[x, h, c], dev(flip=True), core_e_s, core_e_r)
    expo_all[x, h, c] = expo_t[mine, :]
    core_o_s, core_o_r = new_send(own_all.at[0, 0, 0]), new_recv()
    own_all[x, h, c] = own_stats
    push(own_all.at[x, h, c], own_all.at[x, h, c], dev(flip=True), core_o_s, core_o_r)
    nx_s, nx_r = new_send(norm_all.at[0:3, 0]), new_recv()
    for k in RING:
        cols = pl.ds(pl.multiple_of(((x + k) % 4 * 4 + h) * 256, 256), 256)
        push(norm.at[:, cols], norm_all.at[x, c], dev(dx=k), nx_s, nx_r)
    norm_all[x, c] = norm[:, pl.ds(pl.multiple_of((x * 4 + h) * 256, 256), 256)]

    pick_s, pick_r = new_send(hr), new_recv()
    for k in range(4):
        part = dot(picks, heads[x, k], ((1,), (0,)))
        for yy in range(4):
            hs[yy, :, 256 * k : 256 * k + 256] = part[8 * yy : 8 * yy + 8].astype(BF16)
    for i, k in enumerate(RING):
        push(hs.at[(y + k) % 4], hr.at[i], dev(dy=k), pick_s, pick_r)

    others_n = others.T.astype(BF16)
    feat_s, feat_r = new_send(fr), [new_recv() for _ in range(4)]

    def start_feat(q):
        for k in range(4):
            part = dot(others_n, heads[q, k], ((1,), (0,)))
            for yy in range(4):
                rows = part[32 * yy : 32 * yy + 32]
                feat[q, yy, :, 256 * k : 256 * k + 256] = rows
                fs[q, yy, :, 256 * k : 256 * k + 256] = rows.astype(BF16)
        for i, k in enumerate(RING):
            push(fs.at[q, (y + k) % 4], fr.at[q, i], dev(dy=k), feat_s, feat_r[q])

    start_feat(0)
    expoz_s, expoz_r = new_send(expo_all.at[0, 0:3]), [new_recv() for _ in Z_CLASS]
    expox_s, expox_r = new_send(expo_all.at[0:3]), [new_recv() for _ in range(4)]

    def spread_expo(j):
        block = expo_all.at[x, order[j]]
        if j:
            wait(expoz_r[j % 3], block)
        for k in RING:
            push(block, block, dev(dx=k), expox_s, expox_r[j])

    wait(core_e_r, expo_all.at[0, 0, 0])

    def push_expo(i):
        push(expo_all.at[x, h], expo_all.at[x, h], dev(dz=Z_CLASS[i]), expoz_s, expoz_r[i])

    push_expo(1)
    push_expo(2)
    spread_expo(0)
    wait(core_o_r, own_all.at[0, 0, 0])
    ownz_s, ownz_r = new_send(own_all.at[0, 0:3]), new_recv()
    for k in Z_CLASS:
        push(own_all.at[x, h], own_all.at[x, h], dev(dz=k), ownz_s, ownz_r)
    start_feat(1)
    summed_stats = combine(stats_1, stats_r, 15)
    stats_r = send_stats(stats_2, summed_stats, [dev(dz=k) for k in Z_CLASS])
    push_expo(0)
    start_feat(2)
    start_feat(3)
    wait(pick_r, hr)
    hx[x] = (hs[y].astype(F32) + hr[0].astype(F32) + hr[1].astype(F32) + hr[2].astype(F32)).astype(BF16)
    pickx_s, pickx_r = new_send(hx.at[0:3]), new_recv()
    for k in RING:
        push(hx.at[x], hx.at[x], dev(dx=k), pickx_s, pickx_r)
    wait(nx_r, norm_all.at[0:3, 0])
    nc_s, nc_r = new_send(norm_all.at[:, 0]), new_recv()
    push(norm_all.at[:, c], norm_all.at[:, c], dev(flip=True), nc_s, nc_r)
    wait(ownz_r, own_all.at[0, 0:3])
    ownx_s, ownx_r = new_send(own_all.at[0:3]), new_recv()
    for k in RING:
        push(own_all.at[x], own_all.at[x], dev(dx=k), ownx_s, ownx_r)
    spread_expo(1)
    spread_expo(2)
    summed_stats = combine(stats_2, stats_r, 3)
    plane_all[x, c] = summed_stats
    core_p_s, core_p_r = new_send(plane_all.at[0, 0]), new_recv()
    push(plane_all.at[x, c], plane_all.at[x, c], dev(flip=True), core_p_s, core_p_r)
    peak = summed_stats[0:1]
    total = summed_stats[1:2] + summed_stats[2:3]
    scale = weight / total

    wait(core_p_r, plane_all.at[0, 0])
    px_s, px_r = new_send(plane_all.at[0:3]), new_recv()
    for k in RING:
        push(plane_all.at[x], plane_all.at[x], dev(dx=k), px_s, px_r)

    swin_s, swin_r = new_send(wr), new_recv()

    def finish_feat(q):
        wait(feat_r[q], fr.at[q])
        summed = factors[:, 3:4] * feat[q, y]
        for i in range(3):
            summed += factors[:, i : i + 1] * fr[q, i].astype(F32)
        rows = hx[q].astype(F32)
        rows = jnp.concatenate([rows[2 * (k // 4) : 2 * (k // 4) + 2] for k in range(16)], axis=0)
        summed -= factors[:, 4:5] * rows
        for k in range(4):
            wo[q, k] = summed[8 * k : 8 * k + 8]
            ws[q, k] = summed[8 * k : 8 * k + 8].astype(BF16)
        for i, k in enumerate((1, 15, 2 if q < 2 else 14)):
            push(ws.at[q, (l + k) % 4], wr.at[q, i], dev(dz=k), swin_s, swin_r)

    coef[...] = jnp.concatenate(
        [scale * jnp.exp(stats_1[i][0:1] - peak) for i in (12, 13, 14, 15)]
        + [scale * summed_stats[1:2], jnp.zeros((123, 128), F32)],
        axis=0,
    ).T
    factors = coef[pl.ds(pl.multiple_of(32 * y, 32), 32), :]
    wait(pickx_r, hx.at[0:3])
    finish_feat(0)
    finish_feat(1)
    finish_feat(2)
    finish_feat(3)

    def grad_block(j):
        hh = order[j]
        wait(expox_r[j], expo_all.at[0:3, hh])
        ids = 512 * dp + 128 * hh + lax.broadcasted_iota(jnp.int32, (128, 256), 0)
        at_targets = ids == both_targets
        whole = jnp.zeros((128, 256), F32)
        for xx in range(4):
            scales, minus = [], []
            for core in range(2):
                plane = plane_all[xx, core]
                per = lane_weights(xx) / (plane[1:2] + plane[2:3])
                scales.append(per * jnp.exp(own_all[xx, hh, core, 0:1] - plane[0:1]))
                minus.append(per * plane[1:2])
            part = jnp.concatenate([expo_all[xx, hh, core].astype(F32) for core in range(2)], axis=1)
            part = part * jnp.concatenate(scales, axis=1)
            part = part - jnp.where(at_targets, jnp.concatenate(minus, axis=1), 0.0)
            rows = jnp.concatenate([norm_all[xx, core] for core in range(2)], axis=0)
            whole += dot(part.astype(BF16), rows, ((1,), (0,)))
        ghead_ref[pl.ds(pl.multiple_of(hh * 128, 128), 128), :] = whole.astype(BF16)

    wait(swin_r, wr)
    got = jnp.concatenate(
        [wo[q, l] + wr[q, 0].astype(F32) + wr[q, 1].astype(F32) + wr[q, 2].astype(F32) for q in range(4)],
        axis=1,
    )
    rows8, inverse = rows_of(y, l)
    row_dots = jnp.mean(got * gain * rows8, axis=-1, keepdims=True)
    exits = inverse * (gain * got - rows8 * (inverse * inverse * row_dots))
    later = [None] * 4
    later[3] = exits[6:8]
    for k in (2, 1, 0):
        later[k] = exits[2 * k : 2 * k + 2] + later[k + 1]
    ts[...] = later[0].astype(BF16)
    plane_s, plane_r = new_send(tr), new_recv()
    for i, k in enumerate(RING):
        push(ts, tr.at[i], dev(dx=k), plane_s, plane_r)
    wait(nc_r, norm_all.at[:, 0])
    wait(ownx_r, own_all.at[0:3])
    wait(px_r, plane_all.at[0:3])
    wait(plane_r, tr)
    above = jnp.zeros((2, D), F32)
    for i, k in enumerate(RING):
        above += jnp.where(x + (4 - k) < 4, 1.0, 0.0) * tr[i].astype(F32)
    for k in range(4):
        value = later[k] + above
        sf[k] = value
        cs[k] = value.astype(BF16)
    class_s, class_r = new_send(cr), new_recv()
    for i, k in enumerate(Z_CLASS):
        push(cs.at[(h + k // 4) % 4], cr.at[i], dev(dz=k), class_s, class_r)
    spread_expo(3)
    for j in range(4):
        grad_block(j)
    wait(class_r, cr)
    result = sf[h] + top_v[...].astype(F32)
    for i in range(3):
        result += cr[i].astype(F32)
    ghid_ref[0] = result.astype(BF16)
    assert counts == {"send": SENDS, "recv": RECVS}
    for sem, ref in sent:
        wait(sem, ref)


def body(hidden, norm_gain, exit_head, targets, loss_numerators, top_grad):
    vmem = pl.BlockSpec(memory_space=pltpu.VMEM)
    where_it_is = pl.BlockSpec(memory_space=pl.ANY)
    return pl.pallas_call(
        kernel,
        out_shape=(
            jax.ShapeDtypeStruct(exit_head.shape, BF16),
            jax.ShapeDtypeStruct(hidden.shape, BF16),
        ),
        in_specs=[where_it_is] * 6,
        out_specs=(vmem, vmem),
        scratch_shapes=[
            pltpu.VMEM((4, 4, 4, 2, D), BF16),
            pltpu.VMEM((1, D), F32),
            pltpu.VMEM((2, D), BF16),
            pltpu.VMEM((128, D), BF16),
            pltpu.VMEM((4, 4, 256, 256), BF16),
            pltpu.VMEM((256, 128), F32),
            pltpu.VMEM((16, 8, 128), F32),
            pltpu.VMEM((4, 8, 128), F32),
            pltpu.VMEM((256, 128), BF16),
            pltpu.VMEM((4, 4, 2, 128, 128), BF16),
            pltpu.VMEM((4, 4, 2, 8, 128), F32),
            pltpu.VMEM((4, 2, 8, 128), F32),
            pltpu.VMEM((4, 2, 128, 256), BF16),
            pltpu.VMEM((128, 128), F32),
            pltpu.VMEM((4, 8, 1024), BF16),
            pltpu.VMEM((3, 8, 1024), BF16),
            pltpu.VMEM((4, 8, 1024), BF16),
            pltpu.VMEM((4, 4, 32, 1024), F32),
            pltpu.VMEM((4, 4, 32, 1024), BF16),
            pltpu.VMEM((4, 3, 32, 1024), BF16),
            pltpu.VMEM((4, 4, 8, 1024), F32),
            pltpu.VMEM((4, 4, 8, 1024), BF16),
            pltpu.VMEM((4, 3, 8, 1024), BF16),
            pltpu.VMEM((2, D), BF16),
            pltpu.VMEM((3, 2, D), BF16),
            pltpu.VMEM((4, 2, D), F32),
            pltpu.VMEM((4, 2, D), BF16),
            pltpu.VMEM((3, 2, D), BF16),
            pltpu.SMEM((64,), jnp.int32),
            pltpu.SMEM((16,), jnp.int32),
            pltpu.SemaphoreType.DMA((SENDS,)),
            pltpu.SemaphoreType.DMA((RECVS,)),
            pltpu.SemaphoreType.DMA((LOCALS,)),
        ],
        compiler_params=pltpu.CompilerParams(
            collective_id=0, has_side_effects=True, vmem_limit_bytes=60 * 1024 * 1024
        ),
        name="exit_head_backward",
    )(hidden, norm_gain.reshape(1, D), exit_head, targets, loss_numerators, top_grad)


def solution(mesh):
    placed = (P("section", "dp", None), P(), P("dp", "section"), P(), P(), P("dp", None))
    return jax.shard_map(
        body,
        mesh=mesh,
        in_specs=placed,
        out_specs=(P("dp", "section"), P("section", "dp", None)),
        check_vma=False,
    )
```

```python
import functools

import jax
import jax.numpy as jnp
from jax import lax
from jax.experimental import pallas as pl
from jax.experimental.pallas import tpu as pltpu
from jax.sharding import PartitionSpec as P

MESH = pl.DeviceIdType.MESH
EXIT_DENOM = 16
EPSILON = 1e-05
F32 = jnp.float32
BF16 = jnp.bfloat16
D = 4096
SENDS = 26
RECVS = 60
LOCALS = 6
Z_WINDOW = (1, 15, 2)
Z_CLASS = (8, 4, 12)
RING = (1, 3, 2)


def dot(a, b, contract):
    return lax.dot_general(a, b, (contract, ((), ())), preferred_element_type=F32)


def kernel(
    hidden_ref, gain_ref, head_ref, targets_ref, nums_ref, top_ref,
    ghead_ref, ghid_ref,
    raw, gain_v, top_v, norm, heads, logits, stats_1, stats_2, expo_t, expo_all, own_all, plane_all, norm_all,
    coef, hs, hr, hx, hw, hwr, far_top, feat, fs, fr, wo, ws, wr, ts, tr, sf, cs, cr,
    targets_s, nums_s, send_sem, recv_sem, local_sem,
):
    sec, dp = lax.axis_index("section"), lax.axis_index("dp")
    x, h = sec // 4, sec % 4
    l, y, c = dp // 8, (dp // 2) % 4, dp % 2
    z = 4 * h + l

    def dev(dx=0, dy=0, dz=0, flip=False):
        nx, ny, nz = (x + dx) % 4, (y + dy) % 4, (z + dz) % 16
        nc = 1 - c if flip else c
        return {"section": nx * 4 + nz // 4, "dp": (nz % 4) * 8 + ny * 2 + nc}

    counts = {"send": 0, "recv": 0}
    sent = []

    def new_recv():
        counts["recv"] += 1
        return recv_sem.at[counts["recv"] - 1]

    def new_send(total):
        counts["send"] += 1
        sem = send_sem.at[counts["send"] - 1]
        sent.append((sem, total))
        return sem

    def push(src, dst, where, s_sem, r_sem):
        pltpu.make_async_remote_copy(
            src_ref=src, dst_ref=dst, send_sem=s_sem, recv_sem=r_sem,
            device_id=where, device_id_type=MESH,
        ).start()

    def wait(sem, total):
        pltpu.make_async_copy(total, total, sem).wait()

    mine = pl.ds(pl.multiple_of(c * 128, 128), 128)
    other = pl.ds(pl.multiple_of((1 - c) * 128, 128), 128)

    halves = [pl.ds(pl.multiple_of(c * 128 + 64 * k, 64), 64) for k in range(2)]

    def quarter(hh):
        return head_ref.at[pl.ds(pl.multiple_of(hh * 128, 128), 128)]

    locals_ = [
        pltpu.make_async_copy(src, dst, local_sem.at[i])
        for i, (src, dst) in enumerate((
            (hidden_ref.at[0], raw.at[y, l, h]),
            (quarter(h), heads.at[x, h, mine]),
            (gain_ref, gain_v),
            (targets_ref, targets_s),
            (nums_ref, nums_s),
            (top_ref, top_v),
        ))
    ]
    for copy in locals_:
        copy.start()

    barrier = pltpu.get_barrier_semaphore()
    near_z = (1, 15, 2, 14)
    partners = [dev(dz=k) for k in Z_CLASS + near_z] + [dev(dx=k) for k in RING] + [dev(flip=True)]
    partners += [dev(dy=k) for k in RING] + [dev(dy=i, dz=k) for i in RING for k in near_z]
    for where in partners:
        pl.semaphore_signal(barrier, inc=1, device_id=where, device_id_type=MESH)
    pl.semaphore_wait(barrier, len(partners))

    class_pieces = [new_recv() for _ in Z_CLASS]
    window_pieces = [[new_recv() for _ in range(3)] for _ in range(4)]
    ring_pieces = [new_recv() for _ in RING]
    classp_s, windowp_s, ringp_s = new_send(raw.at[0, 0, 0:3]), new_send(raw.at[0, 0:3]), new_send(raw.at[0:3])
    cols_a, cols_b = pl.ds(0, D // 2), pl.ds(D // 2, D // 2)
    mine_now = hidden_ref.at[0]
    for k, sem in zip(Z_CLASS, class_pieces):
        push(mine_now, raw.at[y, l, h], dev(dz=k), classp_s, sem)

    def to_window(src, slot, sems):
        push(src, slot, dev(dz=1), windowp_s, sems[0])
        push(src, slot, dev(dz=15), windowp_s, sems[1])
        push(src.at[:, cols_a], slot.at[:, cols_a], dev(dz=2), windowp_s, sems[2])
        push(src.at[:, cols_b], slot.at[:, cols_b], dev(dz=14), windowp_s, sems[2])

    def to_ring(src, slot):
        for k, sem in zip(RING, ring_pieces):
            push(src, slot, dev(dy=k), ringp_s, sem)

    to_window(mine_now, raw.at[y, l, h], window_pieces[0])
    to_ring(mine_now, raw.at[y, l, h])
    headz_s, headz_r = new_send(heads.at[0, 0:3, 0:128]), [new_recv() for _ in range(6)]

    def transpose(which):
        for i in which:
            k = Z_CLASS[i]
            part = (h + k // 4) % 4 * 128
            for half in range(2):
                rows = pl.ds(pl.multiple_of(part + 64 * half, 64), 64)
                push(head_ref.at[rows], heads.at[x, h, halves[half]], dev(dz=k), headz_s, headz_r[2 * i + half])

    transpose((1, 2))
    headx_s, headx_r = new_send(heads.at[0:3, :, 0:128]), [new_recv() for _ in range(4)]

    def spread(hh, sem):
        block = heads.at[x, hh, mine]
        for k in RING:
            push(block, block, dev(dx=k), headx_s, sem)

    locals_[1].wait()
    spread(h, headx_r[0])
    for i in (0, 2, 3, 4, 5):
        locals_[i].wait()

    lane = lax.broadcasted_iota(jnp.int32, (1, 128), 1)
    lane_y, lane_l, lane_h, lane_r = lane // 32, (lane // 8) % 4, (lane // 2) % 4, lane % 2
    row_of = lane_l * 16 + lane_y * 4 + lane_r
    def lane_targets(core):
        found = jnp.zeros((1, 128), jnp.int32)
        for k in range(64):
            if (k // 2) % 2 == 0:
                found = jnp.where(row_of == k, targets_s[k + 2 * core], found)
        return found

    def lane_weights(plane):
        found = jnp.zeros((1, 128), F32)
        for k in range(4):
            found = jnp.where(lane_h == k, nums_s[plane * 4 + k].astype(F32) / EXIT_DENOM, found)
        return found

    target, weight = lane_targets(c), lane_weights(x)
    both_targets = jnp.concatenate([lane_targets(0), lane_targets(1)], axis=1)
    slot = lax.broadcasted_iota(jnp.int32, (32, 1), 0)
    target_col = jnp.zeros((32, 1), jnp.int32)
    for k in range(32):
        target_col = jnp.where(slot == k, targets_s[(k // 2) % 4 * 16 + k // 8 * 4 + k % 2 + 2 * c], target_col)
    first_id = 1024 * (l * 4 + y) + 128 * h
    lane_id = lax.broadcasted_iota(jnp.int32, (1, 256), 1)
    picks = jnp.where(first_id + lane_id + 384 * (lane_id // 128) == target_col, 1.0, 0.0).astype(BF16)

    def from_window(i, steps):
        for n, k in enumerate((1, 15)):
            slot = raw.at[y, (l - k) % 4, (((z - k) % 16) // 4 - steps) % 4]
            wait(window_pieces[i][n], slot)
            to_ring(slot, slot)

    def from_far(i, steps):
        wait(window_pieces[i][2], raw.at[0, 0, 0])
        for k, cols in ((2, cols_a), (14, cols_b)):
            slot = raw.at[y, (l + 2) % 4, (((z - k) % 16) // 4 - steps) % 4, :, cols]
            for kk, sem in zip(RING, ring_pieces):
                push(slot, slot, dev(dy=kk), ringp_s, sem)

    def from_class(i, steps):
        slot = raw.at[y, l, (h - steps) % 4]
        wait(class_pieces[i], slot)
        to_window(slot, slot, window_pieces[i + 1])
        to_ring(slot, slot)

    order = [h] + [(h - k // 4) % 4 for k in Z_CLASS[1:] + Z_CLASS[:1]]

    def from_head(j):
        for half in range(2):
            block = heads.at[x, order[j], halves[half]]
            wait(headz_r[2 * (j % 3) + half], block)
            for k in RING:
                push(block, block, dev(dx=k), headx_s, headx_r[j])

    from_window(0, 0)
    from_far(0, 0)
    from_class(1, 1)
    from_class(2, 3)
    from_class(0, 2)
    transpose((0,))
    from_head(1)
    from_head(2)
    from_window(2, 1)
    from_window(3, 3)
    from_far(2, 1)
    from_far(3, 3)
    from_window(1, 2)
    from_far(1, 2)
    gain = gain_v[...]

    def rows_of(yy, ll):
        rows = jnp.concatenate([raw[yy, ll, k].astype(F32) for k in range(4)], axis=0)
        return rows, lax.rsqrt(jnp.mean(rows * rows, axis=-1, keepdims=True) + EPSILON)

    def assemble(yy):
        for half in range(2):
            both = []
            for ll in (2 * half, 2 * half + 1):
                rows, inverse = rows_of(yy, ll)
                both.append(rows * inverse * gain)
            at = pl.ds(pl.multiple_of(yy * 32 + half * 16, 16), 16)
            norm[at, :] = jnp.concatenate(both, axis=0).astype(BF16)

    assemble(y)
    from_head(3)
    for k, sem in zip(RING, ring_pieces):
        wait(sem, raw.at[0])
        assemble((y - k) % 4)

    core_s, core_r = new_send(heads.at[:, :, 0:128]), [new_recv() for _ in range(4)]
    logits[...] = jnp.zeros((256, 128), F32)
    for j, hh in enumerate(order):
        wait(headx_r[j], heads.at[0:3, hh, mine])
        block = heads.at[:, hh, mine]
        push(block, block, dev(flip=True), core_s, core_r[j])
        wait(core_r[j], block)
        part = jnp.zeros((256, 128), F32)
        for k in range(4):
            cols = pl.ds(pl.multiple_of((k * 4 + hh) * 256, 256), 256)
            part += dot(heads[k, hh], norm[:, cols], ((1,), (1,)))
        logits[...] += part
    values = logits[...]
    row = lax.broadcasted_iota(jnp.int32, (256, 128), 0)
    at_target = first_id + row + 384 * (row // 128) == target
    first_peak = jnp.max(values, axis=0, keepdims=True)
    expo = jnp.exp(values - first_peak)
    others = jnp.where(at_target, 0.0, expo)
    others_n = others.T.astype(BF16)
    feat_s, feat_r = new_send(fr), [new_recv() for _ in range(4)]

    def start_feat(q):
        for k in range(4):
            part = dot(others_n, heads[q, k], ((1,), (0,)))
            for yy in range(4):
                rows = part[32 * yy : 32 * yy + 32]
                feat[q, yy, :, 256 * k : 256 * k + 256] = rows
                fs[q, yy, :, 256 * k : 256 * k + 256] = rows.astype(BF16)
        for i, k in enumerate(RING):
            push(fs.at[q, (y + k) % 4], fr.at[q, i], dev(dy=k), feat_s, feat_r[q])

    start_feat(0)

    expo_t[...] = others.astype(BF16)
    core_e_s, core_e_r = new_send(expo_all.at[0, 0, 0]), new_recv()
    push(expo_t.at[other], expo_all.at[x, h, c], dev(flip=True), core_e_s, core_e_r)
    expo_all[x, h, c] = expo_t[mine, :]
    expoz_s, expoz_r = new_send(expo_all.at[0, 0:3]), [new_recv() for _ in Z_CLASS]
    expox_s, expox_r = new_send(expo_all.at[0:3]), [new_recv() for _ in range(4)]

    def spread_expo(j):
        block = expo_all.at[x, order[j]]
        if j:
            wait(expoz_r[j % 3], block)
        for k in RING:
            push(block, block, dev(dx=k), expox_s, expox_r[j])


    own_stats = jnp.concatenate(
        [
            first_peak,
            jnp.sum(others, axis=0, keepdims=True),
            jnp.sum(jnp.where(at_target, expo, 0.0), axis=0, keepdims=True),
            jnp.zeros((5, 128), F32),
        ],
        axis=0,
    )

    def send_stats(stats, mine_now, peers):
        n = len(peers)
        s_sem, r_sem = new_send(stats.at[0:n]), new_recv()
        stats[n] = mine_now
        for i, where in enumerate(peers):
            push(stats.at[n], stats.at[i], where, s_sem, r_sem)
        return r_sem

    def combine(stats, r_sem, n):
        wait(r_sem, stats.at[0:n])
        parts = [stats[i] for i in range(n + 1)]
        top = functools.reduce(jnp.maximum, [part[0:1] for part in parts])
        sums = sum(part[1:3] * jnp.exp(part[0:1] - top) for part in parts)
        return jnp.concatenate([top, sums, jnp.zeros((5, 128), F32)], axis=0)

    peers = [dev(dy=i, dz=k) for k in Z_WINDOW + (0,) for i in RING + (0,)][:-1]
    stats_r = send_stats(stats_1, own_stats, peers)
    wait(core_e_r, expo_all.at[0, 0, 0])

    def push_expo(i):
        push(expo_all.at[x, h], expo_all.at[x, h], dev(dz=Z_CLASS[i]), expoz_s, expoz_r[i])

    push_expo(1)
    push_expo(2)
    start_feat(1)
    pick_s, pick_r = new_send(hr), new_recv()
    for k in range(4):
        part = dot(picks, heads[x, k], ((1,), (0,)))
        for yy in range(4):
            hs[yy, :, 256 * k : 256 * k + 256] = part[8 * yy : 8 * yy + 8].astype(BF16)
    for i, k in enumerate(RING):
        push(hs.at[(y + k) % 4], hr.at[i], dev(dy=k), pick_s, pick_r)
    spread_expo(0)
    start_feat(2)

    core_o_s, core_o_r = new_send(own_all.at[0, 0, 0]), new_recv()
    own_all[x, h, c] = own_stats
    push(own_all.at[x, h, c], own_all.at[x, h, c], dev(flip=True), core_o_s, core_o_r)
    summed_stats = combine(stats_1, stats_r, 15)
    stats_r = send_stats(stats_2, summed_stats, [dev(dz=k) for k in Z_CLASS])
    start_feat(3)
    wait(core_o_r, own_all.at[0, 0, 0])
    ownz_s, ownz_r = new_send(own_all.at[0, 0:3]), new_recv()
    for k in Z_CLASS:
        push(own_all.at[x, h], own_all.at[x, h], dev(dz=k), ownz_s, ownz_r)
    push_expo(0)
    nx_s, nx_r = new_send(norm_all.at[0:3, 0]), new_recv()
    for k in RING:
        cols = pl.ds(pl.multiple_of(((x + k) % 4 * 4 + h) * 256, 256), 256)
        push(norm.at[:, cols], norm_all.at[x, c], dev(dx=k), nx_s, nx_r)
    norm_all[x, c] = norm[:, pl.ds(pl.multiple_of((x * 4 + h) * 256, 256), 256)]
    wait(pick_r, hr)
    hx[x] = (hs[y].astype(F32) + hr[0].astype(F32) + hr[1].astype(F32) + hr[2].astype(F32)).astype(BF16)
    pickx_s, pickx_r = new_send(hx.at[0:3]), new_recv()
    for k in RING:
        push(hx.at[x], hx.at[x], dev(dx=k), pickx_s, pickx_r)
    wait(nx_r, norm_all.at[0:3, 0])
    nc_s, nc_r = new_send(norm_all.at[:, 0]), new_recv()
    push(norm_all.at[:, c], norm_all.at[:, c], dev(flip=True), nc_s, nc_r)
    tops = [
        functools.reduce(jnp.maximum, [stats_1[4 * i + k][0:1] for k in range(4)]) for i in range(4)
    ]

    far_s, far_r = new_send(far_top.at[0]), new_recv()
    far_top[0] = jnp.broadcast_to(tops[3], (8, 128))
    push(far_top.at[0], far_top.at[1], dev(dz=14), far_s, far_r)

    def as_rows(lanes, at, size):
        blank = jnp.zeros((128 - len(lanes), 128), F32)
        coef[...] = jnp.concatenate(lanes + [blank], axis=0).T
        return coef[pl.ds(pl.multiple_of(at, size), size), :]

    shares = as_rows([jnp.exp(stats_1[12 + i][0:1] - tops[3]) for i in range(4)], 32 * y, 32)
    swin_s, swin_r = new_send(wr), new_recv()

    def finish_feat(q):
        wait(feat_r[q], fr.at[q])
        summed = shares[:, 3:4] * feat[q, y]
        for i in range(3):
            summed += shares[:, i : i + 1] * fr[q, i].astype(F32)
        for k in range(4):
            wo[q, k] = summed[8 * k : 8 * k + 8]
            ws[q, k] = summed[8 * k : 8 * k + 8].astype(BF16)
        for i, k in enumerate((1, 15, 2 if q < 2 else 14)):
            push(ws.at[q, (l + k) % 4], wr.at[q, i], dev(dz=k), swin_s, swin_r)

    wait(pickx_r, hx.at[0:3])
    picked = jnp.concatenate([hx[q].astype(F32) for q in range(4)], axis=1)
    for k in range(4):
        hw[k] = picked[2 * k : 2 * k + 2].astype(BF16)
    hw_s, hw_r = new_send(hwr), new_recv()
    for i, k in enumerate((1, 15)):
        push(hw.at[(l + k) % 4], hwr.at[i], dev(dz=k), hw_s, hw_r)
    for k, cols in ((2, cols_a), (14, cols_b)):
        push(hw.at[(l + 2) % 4, :, cols], hwr.at[2, :, cols], dev(dz=k), hw_s, hw_r)
    finish_feat(0)
    spread_expo(1)
    spread_expo(2)
    finish_feat(1)
    finish_feat(2)
    finish_feat(3)
    summed_stats = combine(stats_2, stats_r, 3)
    plane_all[x, c] = summed_stats
    core_p_s, core_p_r = new_send(plane_all.at[0, 0]), new_recv()
    push(plane_all.at[x, c], plane_all.at[x, c], dev(flip=True), core_p_s, core_p_r)
    peak = summed_stats[0:1]
    total = summed_stats[1:2] + summed_stats[2:3]
    scale = weight / total

    wait(core_p_r, plane_all.at[0, 0])
    px_s, px_r = new_send(plane_all.at[0:3]), new_recv()
    for k in RING:
        push(plane_all.at[x], plane_all.at[x], dev(dx=k), px_s, px_r)

    wait(far_r, far_top.at[1])
    spreads = [scale * jnp.exp(top - peak) for top in tops + [far_top[1, 0:1]]]
    factors = as_rows(spreads + [scale * summed_stats[1:2]], 32 * y + 8 * l, 8)

    def grad_block(j):
        hh = order[j]
        wait(expox_r[j], expo_all.at[0:3, hh])
        ids = 512 * dp + 128 * hh + lax.broadcasted_iota(jnp.int32, (128, 256), 0)
        at_targets = ids == both_targets
        whole = jnp.zeros((128, 256), F32)
        for xx in range(4):
            scales, minus = [], []
            for core in range(2):
                plane = plane_all[xx, core]
                per = lane_weights(xx) / (plane[1:2] + plane[2:3])
                scales.append(per * jnp.exp(own_all[xx, hh, core, 0:1] - plane[0:1]))
                minus.append(per * plane[1:2])
            part = jnp.concatenate([expo_all[xx, hh, core].astype(F32) for core in range(2)], axis=1)
            part = part * jnp.concatenate(scales, axis=1)
            part = part - jnp.where(at_targets, jnp.concatenate(minus, axis=1), 0.0)
            rows = jnp.concatenate([norm_all[xx, core] for core in range(2)], axis=0)
            whole += dot(part.astype(BF16), rows, ((1,), (0,)))
        ghead_ref[pl.ds(pl.multiple_of(hh * 128, 128), 128), :] = whole.astype(BF16)

    wait(swin_r, wr)
    wait(hw_r, hwr)
    got = factors[:, 3:4] * jnp.concatenate([wo[q, l] for q in range(4)], axis=1)
    for i in range(3):
        halves_in = [jnp.concatenate([wr[q, i], wr[q + 1, i]], axis=1).astype(F32) for q in (0, 2)]
        later_one = 4 if i == 2 else i
        got += jnp.concatenate(
            [factors[:, i : i + 1] * halves_in[0], factors[:, later_one : later_one + 1] * halves_in[1]], axis=1
        )
    rows2 = hw[l].astype(F32) + hwr[0].astype(F32) + hwr[1].astype(F32) + hwr[2].astype(F32)
    got -= factors[:, 5:6] * jnp.concatenate([rows2] * 4, axis=0)
    rows8, inverse = rows_of(y, l)
    row_dots = jnp.mean(got * gain * rows8, axis=-1, keepdims=True)
    exits = inverse * (gain * got - rows8 * (inverse * inverse * row_dots))
    later = [None] * 4
    later[3] = exits[6:8]
    for k in (2, 1, 0):
        later[k] = exits[2 * k : 2 * k + 2] + later[k + 1]
    ts[...] = later[0].astype(BF16)
    plane_s, plane_r = new_send(tr), new_recv()
    for i, k in enumerate(RING):
        push(ts, tr.at[i], dev(dx=k), plane_s, plane_r)
    wait(plane_r, tr)
    above = jnp.zeros((2, D), F32)
    for i, k in enumerate(RING):
        above += jnp.where(x + (4 - k) < 4, 1.0, 0.0) * tr[i].astype(F32)
    for k in range(4):
        value = later[k] + above
        sf[k] = value
        cs[k] = value.astype(BF16)
    class_s, class_r = new_send(cr), new_recv()
    for i, k in enumerate(Z_CLASS):
        push(cs.at[(h + k // 4) % 4], cr.at[i], dev(dz=k), class_s, class_r)
    wait(ownz_r, own_all.at[0, 0:3])
    ownx_s, ownx_r = new_send(own_all.at[0:3]), new_recv()
    for k in RING:
        push(own_all.at[x], own_all.at[x], dev(dx=k), ownx_s, ownx_r)
    spread_expo(3)
    wait(nc_r, norm_all.at[:, 0])
    wait(ownx_r, own_all.at[0:3])
    wait(px_r, plane_all.at[0:3])
    for j in range(4):
        grad_block(j)
    wait(class_r, cr)
    result = sf[h] + top_v[...].astype(F32)
    for i in range(3):
        result += cr[i].astype(F32)
    ghid_ref[0] = result.astype(BF16)
    assert counts == {"send": SENDS, "recv": RECVS}
    for sem, ref in sent:
        wait(sem, ref)


def body(hidden, norm_gain, exit_head, targets, loss_numerators, top_grad):
    vmem = pl.BlockSpec(memory_space=pltpu.VMEM)
    where_it_is = pl.BlockSpec(memory_space=pl.ANY)
    return pl.pallas_call(
        kernel,
        out_shape=(
            jax.ShapeDtypeStruct(exit_head.shape, BF16),
            jax.ShapeDtypeStruct(hidden.shape, BF16),
        ),
        in_specs=[where_it_is] * 6,
        out_specs=(vmem, vmem),
        scratch_shapes=[
            pltpu.VMEM((4, 4, 4, 2, D), BF16),
            pltpu.VMEM((1, D), F32),
            pltpu.VMEM((2, D), BF16),
            pltpu.VMEM((128, D), BF16),
            pltpu.VMEM((4, 4, 256, 256), BF16),
            pltpu.VMEM((256, 128), F32),
            pltpu.VMEM((16, 8, 128), F32),
            pltpu.VMEM((4, 8, 128), F32),
            pltpu.VMEM((256, 128), BF16),
            pltpu.VMEM((4, 4, 2, 128, 128), BF16),
            pltpu.VMEM((4, 4, 2, 8, 128), F32),
            pltpu.VMEM((4, 2, 8, 128), F32),
            pltpu.VMEM((4, 2, 128, 256), BF16),
            pltpu.VMEM((128, 128), F32),
            pltpu.VMEM((4, 8, 1024), BF16),
            pltpu.VMEM((3, 8, 1024), BF16),
            pltpu.VMEM((4, 8, 1024), BF16),
            pltpu.VMEM((4, 2, D), BF16),
            pltpu.VMEM((3, 2, D), BF16),
            pltpu.VMEM((2, 8, 128), F32),
            pltpu.VMEM((4, 4, 32, 1024), F32),
            pltpu.VMEM((4, 4, 32, 1024), BF16),
            pltpu.VMEM((4, 3, 32, 1024), BF16),
            pltpu.VMEM((4, 4, 8, 1024), F32),
            pltpu.VMEM((4, 4, 8, 1024), BF16),
            pltpu.VMEM((4, 3, 8, 1024), BF16),
            pltpu.VMEM((2, D), BF16),
            pltpu.VMEM((3, 2, D), BF16),
            pltpu.VMEM((4, 2, D), F32),
            pltpu.VMEM((4, 2, D), BF16),
            pltpu.VMEM((3, 2, D), BF16),
            pltpu.SMEM((64,), jnp.int32),
            pltpu.SMEM((16,), jnp.int32),
            pltpu.SemaphoreType.DMA((SENDS,)),
            pltpu.SemaphoreType.DMA((RECVS,)),
            pltpu.SemaphoreType.DMA((LOCALS,)),
        ],
        compiler_params=pltpu.CompilerParams(
            collective_id=0, has_side_effects=True, vmem_limit_bytes=60 * 1024 * 1024
        ),
        name="exit_head_backward",
    )(hidden, norm_gain.reshape(1, D), exit_head, targets, loss_numerators, top_grad)


def solution(mesh):
    placed = (P("section", "dp", None), P(), P("dp", "section"), P(), P(), P("dp", None))
    return jax.shard_map(
        body,
        mesh=mesh,
        in_specs=placed,
        out_specs=(P("dp", "section"), P("section", "dp", None)),
        check_vma=False,
    )
```

```python
import functools

import jax
import jax.numpy as jnp
from jax import lax
from jax.experimental import pallas as pl
from jax.experimental.pallas import tpu as pltpu
from jax.sharding import PartitionSpec as P

MESH = pl.DeviceIdType.MESH
EXIT_DENOM = 16
EPSILON = 1e-05
F32 = jnp.float32
BF16 = jnp.bfloat16
D = 4096
SENDS = 26
RECVS = 60
LOCALS = 6
Z_WINDOW = (1, 15, 2)
Z_CLASS = (8, 4, 12)
RING = (1, 3, 2)


def dot(a, b, contract):
    return lax.dot_general(a, b, (contract, ((), ())), preferred_element_type=F32)


def kernel(
    hidden_ref, gain_ref, head_ref, targets_ref, nums_ref, top_ref,
    ghead_ref, ghid_ref,
    raw, gain_v, top_v, norm, heads, logits, stats_1, stats_2, expo_t, expo_all, own_all, plane_all, norm_all,
    coef, hs, hr, hx, hw, hwr, far_top, feat, fs, fr, wo, ws, wr, ts, tr, sf, cs, cr,
    targets_s, nums_s, send_sem, recv_sem, local_sem,
):
    sec, dp = lax.axis_index("section"), lax.axis_index("dp")
    x, h = sec // 4, sec % 4
    l, y, c = dp // 8, (dp // 2) % 4, dp % 2
    z = 4 * h + l

    def dev(dx=0, dy=0, dz=0, flip=False):
        nx, ny, nz = (x + dx) % 4, (y + dy) % 4, (z + dz) % 16
        nc = 1 - c if flip else c
        return {"section": nx * 4 + nz // 4, "dp": (nz % 4) * 8 + ny * 2 + nc}

    counts = {"send": 0, "recv": 0}
    sent = []

    def new_recv():
        counts["recv"] += 1
        return recv_sem.at[counts["recv"] - 1]

    def new_send(total):
        counts["send"] += 1
        sem = send_sem.at[counts["send"] - 1]
        sent.append((sem, total))
        return sem

    def push(src, dst, where, s_sem, r_sem):
        pltpu.make_async_remote_copy(
            src_ref=src, dst_ref=dst, send_sem=s_sem, recv_sem=r_sem,
            device_id=where, device_id_type=MESH,
        ).start()

    def wait(sem, total):
        pltpu.make_async_copy(total, total, sem).wait()

    mine = pl.ds(pl.multiple_of(c * 128, 128), 128)
    other = pl.ds(pl.multiple_of((1 - c) * 128, 128), 128)

    halves = [pl.ds(pl.multiple_of(c * 128 + 64 * k, 64), 64) for k in range(2)]

    def quarter(hh):
        return head_ref.at[pl.ds(pl.multiple_of(hh * 128, 128), 128)]

    locals_ = [
        pltpu.make_async_copy(src, dst, local_sem.at[i])
        for i, (src, dst) in enumerate((
            (hidden_ref.at[0], raw.at[y, l, h]),
            (quarter(h), heads.at[x, h, mine]),
            (gain_ref, gain_v),
            (targets_ref, targets_s),
            (nums_ref, nums_s),
            (top_ref, top_v),
        ))
    ]
    for copy in locals_:
        copy.start()

    barrier = pltpu.get_barrier_semaphore()
    near_z = (1, 15, 2, 14)
    partners = [dev(dz=k) for k in Z_CLASS + near_z] + [dev(dx=k) for k in RING] + [dev(flip=True)]
    partners += [dev(dy=k) for k in RING] + [dev(dy=i, dz=k) for i in RING for k in near_z]
    for where in partners:
        pl.semaphore_signal(barrier, inc=1, device_id=where, device_id_type=MESH)
    pl.semaphore_wait(barrier, len(partners))

    class_pieces = [new_recv() for _ in Z_CLASS]
    window_pieces = [[new_recv() for _ in range(3)] for _ in range(4)]
    ring_pieces = [new_recv() for _ in RING]
    classp_s, windowp_s, ringp_s = new_send(raw.at[0, 0, 0:3]), new_send(raw.at[0, 0:3]), new_send(raw.at[0:3])
    cols_a, cols_b = pl.ds(0, D // 2), pl.ds(D // 2, D // 2)
    mine_now = hidden_ref.at[0]
    for k, sem in zip(Z_CLASS, class_pieces):
        push(mine_now, raw.at[y, l, h], dev(dz=k), classp_s, sem)

    def to_window(src, slot, sems):
        push(src, slot, dev(dz=1), windowp_s, sems[0])
        push(src, slot, dev(dz=15), windowp_s, sems[1])
        push(src.at[:, cols_a], slot.at[:, cols_a], dev(dz=2), windowp_s, sems[2])
        push(src.at[:, cols_b], slot.at[:, cols_b], dev(dz=14), windowp_s, sems[2])

    def to_ring(src, slot):
        for k, sem in zip(RING, ring_pieces):
            push(src, slot, dev(dy=k), ringp_s, sem)

    to_window(mine_now, raw.at[y, l, h], window_pieces[0])
    to_ring(mine_now, raw.at[y, l, h])
    headz_s, headz_r = new_send(heads.at[0, 0:3, 0:128]), [new_recv() for _ in range(6)]

    def transpose(which):
        for i in which:
            k = Z_CLASS[i]
            part = (h + k // 4) % 4 * 128
            for half in range(2):
                rows = pl.ds(pl.multiple_of(part + 64 * half, 64), 64)
                push(head_ref.at[rows], heads.at[x, h, halves[half]], dev(dz=k), headz_s, headz_r[2 * i + half])

    headx_s, headx_r = new_send(heads.at[0:3, :, 0:128]), [new_recv() for _ in range(4)]

    def spread(hh, sem):
        block = heads.at[x, hh, mine]
        for k in RING:
            push(block, block, dev(dx=k), headx_s, sem)

    locals_[1].wait()
    spread(h, headx_r[0])
    for i in (0, 2, 3, 4, 5):
        locals_[i].wait()

    lane = lax.broadcasted_iota(jnp.int32, (1, 128), 1)
    lane_y, lane_l, lane_h, lane_r = lane // 32, (lane // 8) % 4, (lane // 2) % 4, lane % 2
    row_of = lane_l * 16 + lane_y * 4 + lane_r
    def lane_targets(core):
        found = jnp.zeros((1, 128), jnp.int32)
        for k in range(64):
            if (k // 2) % 2 == 0:
                found = jnp.where(row_of == k, targets_s[k + 2 * core], found)
        return found

    def lane_weights(plane):
        found = jnp.zeros((1, 128), F32)
        for k in range(4):
            found = jnp.where(lane_h == k, nums_s[plane * 4 + k].astype(F32) / EXIT_DENOM, found)
        return found

    target, weight = lane_targets(c), lane_weights(x)
    both_targets = jnp.concatenate([lane_targets(0), lane_targets(1)], axis=1)
    slot = lax.broadcasted_iota(jnp.int32, (32, 1), 0)
    target_col = jnp.zeros((32, 1), jnp.int32)
    for k in range(32):
        target_col = jnp.where(slot == k, targets_s[(k // 2) % 4 * 16 + k // 8 * 4 + k % 2 + 2 * c], target_col)
    first_id = 1024 * (l * 4 + y) + 128 * h
    lane_id = lax.broadcasted_iota(jnp.int32, (1, 256), 1)
    picks = jnp.where(first_id + lane_id + 384 * (lane_id // 128) == target_col, 1.0, 0.0).astype(BF16)

    def from_window(i, steps):
        for n, k in enumerate((1, 15)):
            slot = raw.at[y, (l - k) % 4, (((z - k) % 16) // 4 - steps) % 4]
            wait(window_pieces[i][n], slot)
            to_ring(slot, slot)

    def from_far(i, steps):
        wait(window_pieces[i][2], raw.at[0, 0, 0])
        for k, cols in ((2, cols_a), (14, cols_b)):
            slot = raw.at[y, (l + 2) % 4, (((z - k) % 16) // 4 - steps) % 4, :, cols]
            for kk, sem in zip(RING, ring_pieces):
                push(slot, slot, dev(dy=kk), ringp_s, sem)

    def from_class(i, steps):
        slot = raw.at[y, l, (h - steps) % 4]
        wait(class_pieces[i], slot)
        to_window(slot, slot, window_pieces[i + 1])
        to_ring(slot, slot)

    order = [h] + [(h - k // 4) % 4 for k in Z_CLASS[1:] + Z_CLASS[:1]]

    def from_head(j):
        for half in range(2):
            block = heads.at[x, order[j], halves[half]]
            wait(headz_r[2 * (j % 3) + half], block)
            for k in RING:
                push(block, block, dev(dx=k), headx_s, headx_r[j])

    transpose((1, 2))
    from_window(0, 0)
    from_far(0, 0)
    from_class(1, 1)
    from_class(2, 3)
    from_class(0, 2)
    transpose((0,))
    from_head(1)
    from_head(2)
    from_window(2, 1)
    from_window(3, 3)
    from_far(2, 1)
    from_far(3, 3)
    from_window(1, 2)
    from_far(1, 2)
    gain = gain_v[...]

    def rows_of(yy, ll):
        rows = jnp.concatenate([raw[yy, ll, k].astype(F32) for k in range(4)], axis=0)
        return rows, lax.rsqrt(jnp.mean(rows * rows, axis=-1, keepdims=True) + EPSILON)

    def assemble(yy):
        for half in range(2):
            both = []
            for ll in (2 * half, 2 * half + 1):
                rows, inverse = rows_of(yy, ll)
                both.append(rows * inverse * gain)
            at = pl.ds(pl.multiple_of(yy * 32 + half * 16, 16), 16)
            norm[at, :] = jnp.concatenate(both, axis=0).astype(BF16)

    assemble(y)
    from_head(3)
    for k, sem in zip(RING, ring_pieces):
        wait(sem, raw.at[0])
        assemble((y - k) % 4)

    core_s, core_r = new_send(heads.at[:, :, 0:128]), [new_recv() for _ in range(4)]
    logits[...] = jnp.zeros((256, 128), F32)
    for j, hh in enumerate(order):
        wait(headx_r[j], heads.at[0:3, hh, mine])
        block = heads.at[:, hh, mine]
        push(block, block, dev(flip=True), core_s, core_r[j])
        wait(core_r[j], block)
        part = jnp.zeros((256, 128), F32)
        for k in range(4):
            cols = pl.ds(pl.multiple_of((k * 4 + hh) * 256, 256), 256)
            part += dot(heads[k, hh], norm[:, cols], ((1,), (1,)))
        logits[...] += part
    values = logits[...]
    row = lax.broadcasted_iota(jnp.int32, (256, 128), 0)
    at_target = first_id + row + 384 * (row // 128) == target
    first_peak = jnp.max(values, axis=0, keepdims=True)
    expo = jnp.exp(values - first_peak)
    others = jnp.where(at_target, 0.0, expo)
    others_n = others.T.astype(BF16)
    feat_s, feat_r = new_send(fr), [new_recv() for _ in range(4)]

    def start_feat(q):
        for k in range(4):
            part = dot(others_n, heads[q, k], ((1,), (0,)))
            for yy in range(4):
                rows = part[32 * yy : 32 * yy + 32]
                feat[q, yy, :, 256 * k : 256 * k + 256] = rows
                fs[q, yy, :, 256 * k : 256 * k + 256] = rows.astype(BF16)
        for i, k in enumerate(RING):
            push(fs.at[q, (y + k) % 4], fr.at[q, i], dev(dy=k), feat_s, feat_r[q])

    start_feat(0)

    expo_t[...] = others.astype(BF16)
    core_e_s, core_e_r = new_send(expo_all.at[0, 0, 0]), new_recv()
    push(expo_t.at[other], expo_all.at[x, h, c], dev(flip=True), core_e_s, core_e_r)
    expo_all[x, h, c] = expo_t[mine, :]
    expoz_s, expoz_r = new_send(expo_all.at[0, 0:3]), [new_recv() for _ in Z_CLASS]
    expox_s, expox_r = new_send(expo_all.at[0:3]), [new_recv() for _ in range(4)]

    def spread_expo(j):
        block = expo_all.at[x, order[j]]
        if j:
            wait(expoz_r[j % 3], block)
        for k in RING:
            push(block, block, dev(dx=k), expox_s, expox_r[j])


    own_stats = jnp.concatenate(
        [
            first_peak,
            jnp.sum(others, axis=0, keepdims=True),
            jnp.sum(jnp.where(at_target, expo, 0.0), axis=0, keepdims=True),
            jnp.zeros((5, 128), F32),
        ],
        axis=0,
    )

    def send_stats(stats, mine_now, peers):
        n = len(peers)
        s_sem, r_sem = new_send(stats.at[0:n]), new_recv()
        stats[n] = mine_now
        for i, where in enumerate(peers):
            push(stats.at[n], stats.at[i], where, s_sem, r_sem)
        return r_sem

    def combine(stats, r_sem, n):
        wait(r_sem, stats.at[0:n])
        parts = [stats[i] for i in range(n + 1)]
        top = functools.reduce(jnp.maximum, [part[0:1] for part in parts])
        sums = sum(part[1:3] * jnp.exp(part[0:1] - top) for part in parts)
        return jnp.concatenate([top, sums, jnp.zeros((5, 128), F32)], axis=0)

    peers = [dev(dy=i, dz=k) for k in Z_WINDOW + (0,) for i in RING + (0,)][:-1]
    stats_r = send_stats(stats_1, own_stats, peers)
    wait(core_e_r, expo_all.at[0, 0, 0])

    def push_expo(i):
        push(expo_all.at[x, h], expo_all.at[x, h], dev(dz=Z_CLASS[i]), expoz_s, expoz_r[i])

    push_expo(1)
    push_expo(2)
    start_feat(1)
    pick_s, pick_r = new_send(hr), new_recv()
    for k in range(4):
        part = dot(picks, heads[x, k], ((1,), (0,)))
        for yy in range(4):
            hs[yy, :, 256 * k : 256 * k + 256] = part[8 * yy : 8 * yy + 8].astype(BF16)
    for i, k in enumerate(RING):
        push(hs.at[(y + k) % 4], hr.at[i], dev(dy=k), pick_s, pick_r)
    spread_expo(0)
    start_feat(2)

    core_o_s, core_o_r = new_send(own_all.at[0, 0, 0]), new_recv()
    own_all[x, h, c] = own_stats
    push(own_all.at[x, h, c], own_all.at[x, h, c], dev(flip=True), core_o_s, core_o_r)
    summed_stats = combine(stats_1, stats_r, 15)
    stats_r = send_stats(stats_2, summed_stats, [dev(dz=k) for k in Z_CLASS])
    start_feat(3)
    wait(core_o_r, own_all.at[0, 0, 0])
    ownz_s, ownz_r = new_send(own_all.at[0, 0:3]), new_recv()
    for k in Z_CLASS:
        push(own_all.at[x, h], own_all.at[x, h], dev(dz=k), ownz_s, ownz_r)
    push_expo(0)
    nx_s, nx_r = new_send(norm_all.at[0:3, 0]), new_recv()
    for k in RING:
        cols = pl.ds(pl.multiple_of(((x + k) % 4 * 4 + h) * 256, 256), 256)
        push(norm.at[:, cols], norm_all.at[x, c], dev(dx=k), nx_s, nx_r)
    norm_all[x, c] = norm[:, pl.ds(pl.multiple_of((x * 4 + h) * 256, 256), 256)]
    wait(pick_r, hr)
    hx[x] = (hs[y].astype(F32) + hr[0].astype(F32) + hr[1].astype(F32) + hr[2].astype(F32)).astype(BF16)
    pickx_s, pickx_r = new_send(hx.at[0:3]), new_recv()
    for k in RING:
        push(hx.at[x], hx.at[x], dev(dx=k), pickx_s, pickx_r)
    wait(nx_r, norm_all.at[0:3, 0])
    nc_s, nc_r = new_send(norm_all.at[:, 0]), new_recv()
    push(norm_all.at[:, c], norm_all.at[:, c], dev(flip=True), nc_s, nc_r)
    tops = [
        functools.reduce(jnp.maximum, [stats_1[4 * i + k][0:1] for k in range(4)]) for i in range(4)
    ]

    far_s, far_r = new_send(far_top.at[0]), new_recv()
    far_top[0] = jnp.broadcast_to(tops[3], (8, 128))
    push(far_top.at[0], far_top.at[1], dev(dz=14), far_s, far_r)

    def as_rows(lanes, at, size):
        blank = jnp.zeros((128 - len(lanes), 128), F32)
        coef[...] = jnp.concatenate(lanes + [blank], axis=0).T
        return coef[pl.ds(pl.multiple_of(at, size), size), :]

    shares = as_rows([jnp.exp(stats_1[12 + i][0:1] - tops[3]) for i in range(4)], 32 * y, 32)
    swin_s, swin_r = new_send(wr), new_recv()

    def finish_feat(q):
        wait(feat_r[q], fr.at[q])
        summed = shares[:, 3:4] * feat[q, y]
        for i in range(3):
            summed += shares[:, i : i + 1] * fr[q, i].astype(F32)
        for k in range(4):
            wo[q, k] = summed[8 * k : 8 * k + 8]
            ws[q, k] = summed[8 * k : 8 * k + 8].astype(BF16)
        for i, k in enumerate((1, 15, 2 if q < 2 else 14)):
            push(ws.at[q, (l + k) % 4], wr.at[q, i], dev(dz=k), swin_s, swin_r)

    wait(pickx_r, hx.at[0:3])
    picked = jnp.concatenate([hx[q].astype(F32) for q in range(4)], axis=1)
    for k in range(4):
        hw[k] = picked[2 * k : 2 * k + 2].astype(BF16)
    hw_s, hw_r = new_send(hwr), new_recv()
    for i, k in enumerate((1, 15)):
        push(hw.at[(l + k) % 4], hwr.at[i], dev(dz=k), hw_s, hw_r)
    for k, cols in ((2, cols_a), (14, cols_b)):
        push(hw.at[(l + 2) % 4, :, cols], hwr.at[2, :, cols], dev(dz=k), hw_s, hw_r)
    finish_feat(0)
    spread_expo(1)
    spread_expo(2)
    finish_feat(1)
    finish_feat(2)
    finish_feat(3)
    summed_stats = combine(stats_2, stats_r, 3)
    plane_all[x, c] = summed_stats
    core_p_s, core_p_r = new_send(plane_all.at[0, 0]), new_recv()
    push(plane_all.at[x, c], plane_all.at[x, c], dev(flip=True), core_p_s, core_p_r)
    peak = summed_stats[0:1]
    total = summed_stats[1:2] + summed_stats[2:3]
    scale = weight / total

    wait(core_p_r, plane_all.at[0, 0])
    px_s, px_r = new_send(plane_all.at[0:3]), new_recv()
    for k in RING:
        push(plane_all.at[x], plane_all.at[x], dev(dx=k), px_s, px_r)

    wait(far_r, far_top.at[1])
    spreads = [scale * jnp.exp(top - peak) for top in tops + [far_top[1, 0:1]]]
    factors = as_rows(spreads + [scale * summed_stats[1:2]], 32 * y + 8 * l, 8)

    def grad_block(j):
        hh = order[j]
        wait(expox_r[j], expo_all.at[0:3, hh])
        ids = 512 * dp + 128 * hh + lax.broadcasted_iota(jnp.int32, (128, 256), 0)
        at_targets = ids == both_targets
        whole = jnp.zeros((128, 256), F32)
        for xx in range(4):
            scales, minus = [], []
            for core in range(2):
                plane = plane_all[xx, core]
                per = lane_weights(xx) / (plane[1:2] + plane[2:3])
                scales.append(per * jnp.exp(own_all[xx, hh, core, 0:1] - plane[0:1]))
                minus.append(per * plane[1:2])
            part = jnp.concatenate([expo_all[xx, hh, core].astype(F32) for core in range(2)], axis=1)
            part = part * jnp.concatenate(scales, axis=1)
            part = part - jnp.where(at_targets, jnp.concatenate(minus, axis=1), 0.0)
            rows = jnp.concatenate([norm_all[xx, core] for core in range(2)], axis=0)
            whole += dot(part.astype(BF16), rows, ((1,), (0,)))
        ghead_ref[pl.ds(pl.multiple_of(hh * 128, 128), 128), :] = whole.astype(BF16)

    wait(swin_r, wr)
    wait(hw_r, hwr)
    got = factors[:, 3:4] * jnp.concatenate([wo[q, l] for q in range(4)], axis=1)
    for i in range(3):
        halves_in = [jnp.concatenate([wr[q, i], wr[q + 1, i]], axis=1).astype(F32) for q in (0, 2)]
        later_one = 4 if i == 2 else i
        got += jnp.concatenate(
            [factors[:, i : i + 1] * halves_in[0], factors[:, later_one : later_one + 1] * halves_in[1]], axis=1
        )
    rows2 = hw[l].astype(F32) + hwr[0].astype(F32) + hwr[1].astype(F32) + hwr[2].astype(F32)
    got -= factors[:, 5:6] * jnp.concatenate([rows2] * 4, axis=0)
    rows8, inverse = rows_of(y, l)
    row_dots = jnp.mean(got * gain * rows8, axis=-1, keepdims=True)
    exits = inverse * (gain * got - rows8 * (inverse * inverse * row_dots))
    later = [None] * 4
    later[3] = exits[6:8]
    for k in (2, 1, 0):
        later[k] = exits[2 * k : 2 * k + 2] + later[k + 1]
    ts[...] = later[0].astype(BF16)
    plane_s, plane_r = new_send(tr), new_recv()
    for i, k in enumerate(RING):
        push(ts, tr.at[i], dev(dx=k), plane_s, plane_r)
    wait(plane_r, tr)
    above = jnp.zeros((2, D), F32)
    for i, k in enumerate(RING):
        above += jnp.where(x + (4 - k) < 4, 1.0, 0.0) * tr[i].astype(F32)
    for k in range(4):
        value = later[k] + above
        sf[k] = value
        cs[k] = value.astype(BF16)
    class_s, class_r = new_send(cr), new_recv()
    for i, k in enumerate(Z_CLASS):
        push(cs.at[(h + k // 4) % 4], cr.at[i], dev(dz=k), class_s, class_r)
    wait(ownz_r, own_all.at[0, 0:3])
    ownx_s, ownx_r = new_send(own_all.at[0:3]), new_recv()
    for k in RING:
        push(own_all.at[x], own_all.at[x], dev(dx=k), ownx_s, ownx_r)
    spread_expo(3)
    wait(nc_r, norm_all.at[:, 0])
    wait(ownx_r, own_all.at[0:3])
    wait(px_r, plane_all.at[0:3])
    for j in range(4):
        grad_block(j)
    wait(class_r, cr)
    result = sf[h] + top_v[...].astype(F32)
    for i in range(3):
        result += cr[i].astype(F32)
    ghid_ref[0] = result.astype(BF16)
    assert counts == {"send": SENDS, "recv": RECVS}
    for sem, ref in sent:
        wait(sem, ref)


def body(hidden, norm_gain, exit_head, targets, loss_numerators, top_grad):
    vmem = pl.BlockSpec(memory_space=pltpu.VMEM)
    where_it_is = pl.BlockSpec(memory_space=pl.ANY)
    return pl.pallas_call(
        kernel,
        out_shape=(
            jax.ShapeDtypeStruct(exit_head.shape, BF16),
            jax.ShapeDtypeStruct(hidden.shape, BF16),
        ),
        in_specs=[where_it_is] * 6,
        out_specs=(vmem, vmem),
        scratch_shapes=[
            pltpu.VMEM((4, 4, 4, 2, D), BF16),
            pltpu.VMEM((1, D), F32),
            pltpu.VMEM((2, D), BF16),
            pltpu.VMEM((128, D), BF16),
            pltpu.VMEM((4, 4, 256, 256), BF16),
            pltpu.VMEM((256, 128), F32),
            pltpu.VMEM((16, 8, 128), F32),
            pltpu.VMEM((4, 8, 128), F32),
            pltpu.VMEM((256, 128), BF16),
            pltpu.VMEM((4, 4, 2, 128, 128), BF16),
            pltpu.VMEM((4, 4, 2, 8, 128), F32),
            pltpu.VMEM((4, 2, 8, 128), F32),
            pltpu.VMEM((4, 2, 128, 256), BF16),
            pltpu.VMEM((128, 128), F32),
            pltpu.VMEM((4, 8, 1024), BF16),
            pltpu.VMEM((3, 8, 1024), BF16),
            pltpu.VMEM((4, 8, 1024), BF16),
            pltpu.VMEM((4, 2, D), BF16),
            pltpu.VMEM((3, 2, D), BF16),
            pltpu.VMEM((2, 8, 128), F32),
            pltpu.VMEM((4, 4, 32, 1024), F32),
            pltpu.VMEM((4, 4, 32, 1024), BF16),
            pltpu.VMEM((4, 3, 32, 1024), BF16),
            pltpu.VMEM((4, 4, 8, 1024), F32),
            pltpu.VMEM((4, 4, 8, 1024), BF16),
            pltpu.VMEM((4, 3, 8, 1024), BF16),
            pltpu.VMEM((2, D), BF16),
            pltpu.VMEM((3, 2, D), BF16),
            pltpu.VMEM((4, 2, D), F32),
            pltpu.VMEM((4, 2, D), BF16),
            pltpu.VMEM((3, 2, D), BF16),
            pltpu.SMEM((64,), jnp.int32),
            pltpu.SMEM((16,), jnp.int32),
            pltpu.SemaphoreType.DMA((SENDS,)),
            pltpu.SemaphoreType.DMA((RECVS,)),
            pltpu.SemaphoreType.DMA((LOCALS,)),
        ],
        compiler_params=pltpu.CompilerParams(
            collective_id=0, has_side_effects=True, vmem_limit_bytes=60 * 1024 * 1024
        ),
        name="exit_head_backward",
    )(hidden, norm_gain.reshape(1, D), exit_head, targets, loss_numerators, top_grad)


def solution(mesh):
    placed = (P("section", "dp", None), P(), P("dp", "section"), P(), P(), P("dp", None))
    return jax.shard_map(
        body,
        mesh=mesh,
        in_specs=placed,
        out_specs=(P("dp", "section"), P("section", "dp", None)),
        check_vma=False,
    )
```
